256 devices in a mesh: row: 8 (over y, core), col: 32 (over z, x).
Axes of the slice: x: 4, y: 4, z: 8, core: 2. Of those that a mesh axis runs over, the one named last changes fastest.
Arguments:
- queries: bfloat16 [3, 2048, 4096], P(None, 'row', 'col'), may hold values from -32 to 32
- keys: bfloat16 [3, 2048, 4096], P(None, 'row', 'col'), may hold values from -32 to 32
- values: bfloat16 [3, 2048, 4096], P(None, 'row', 'col'), may hold values from -16 to 16
- grad_out: bfloat16 [3, 2048, 4096], P(None, 'row', 'col'), may hold values from -16 to 16
- out_weight: bfloat16 [4096, 4096], P('row', 'col'), may hold values from -0.09375 to 0.09375
- tile_plan: int32 [336, 3], P('row'), may hold values from 0 to 15, as said below
- row_moment: float32 [4096], P('row'), may hold values from 0.5 to 5
- col_moment: float32 [4096], P('col'), may hold values from 0.5 to 5
Outputs:
- query_grad: bfloat16 [3, 2048, 4096], P(None, 'row', 'col')
- key_grad: bfloat16 [3, 2048, 4096], P(None, 'row', 'col')
- value_grad: bfloat16 [3, 2048, 4096], P(None, 'row', 'col')
- weight_update: float32 [4096, 4096], P('row', 'col')
- new_row_moment: float32 [4096], P('row')
- new_col_moment: float32 [4096], P('col')
The draws below stay inside these ranges and needn't reach their ends.
Inputs may be any that keep to these rules, and one draw needn't show every extreme that they name: `tile_plan`: each row is (sequence, query block, key block) of one tile, key block <= query block < 16; no tile appears twice; for each of the 3 sequences the plan holds all 16 diagonal tiles and 112 tiles in all; rows i * 42 to (i + 1) * 42 - 1 are the tiles that index i of row computes.
All inputs are finite; a program needn't handle non-finite values.
Results may differ from the reference program's by a relative error of at most 0.03.
Values may be sent and summed in bfloat16 or wider, within the bound.
No kernel may reach another device: no remote copies, remote signals or barrier semaphores. Data moves between devices by JAX's collectives and lax.ppermute only.
A program may use at most 128 MiB of HBM per device.

```python
import math
import jax
import jax.numpy as jnp
import numpy as np
from jax import lax

D = 4096
HEADS = 64
HEAD_DIM = 64
HD = 4096
LEN = 2048
BLOCK = 128
KEEP = 7
SEQS = 3


def draw_queries(key, part):
    key = jax.random.fold_in(key, 1)
    drawn = jax.random.truncated_normal(key, -3.0, 3.0, (SEQS, LEN, HD), jnp.float32)
    return drawn.astype(jnp.bfloat16)


def draw_keys(key, part):
    key = jax.random.fold_in(key, 2)
    drawn = jax.random.truncated_normal(key, -3.0, 3.0, (SEQS, LEN, HD), jnp.float32)
    return drawn.astype(jnp.bfloat16)


def draw_values(key, part):
    key = jax.random.fold_in(key, 3)
    column = jnp.arange(HD, dtype=jnp.float32) / HD
    rough = jax.random.uniform(jax.random.fold_in(key, 1), (HD,), jnp.float32, -0.4, 0.4)
    scale = 0.6 * 3.0 ** column * jnp.exp(rough)
    entries = jax.random.truncated_normal(key, -4.0, 4.0, (SEQS, LEN, HD), jnp.float32)
    return (entries * scale).astype(jnp.bfloat16)


def draw_grad_out(key, part):
    key = jax.random.fold_in(key, 4)
    column = jnp.arange(D, dtype=jnp.float32) / D
    rough = jax.random.uniform(jax.random.fold_in(key, 1), (D,), jnp.float32, -0.4, 0.4)
    scale = 0.6 * 3.0 ** column * jnp.exp(rough)
    entries = jax.random.truncated_normal(key, -4.0, 4.0, (SEQS, LEN, D), jnp.float32)
    return (entries * scale).astype(jnp.bfloat16)


def draw_tile_plan(key, part):
    key = jax.random.fold_in(key, 11)
    blocks = LEN // BLOCK
    lower = np.array([[upper, inner] for upper in range(blocks) for inner in range(upper)], dtype=np.int32)
    diagonal = np.stack([np.arange(blocks), np.arange(blocks)], axis=1).astype(np.int32)
    extra = (KEEP - 1) * blocks
    pieces = []
    for sequence in range(SEQS):
        order = jax.random.permutation(jax.random.fold_in(key, sequence), lower.shape[0])
        chosen = jnp.take(jnp.asarray(lower), order[:extra], axis=0)
        pairs = jnp.concatenate([jnp.asarray(diagonal), chosen], axis=0)
        label = jnp.full((pairs.shape[0], 1), sequence, jnp.int32)
        pieces.append(jnp.concatenate([label, pairs], axis=1))
    plan = jnp.concatenate(pieces, axis=0)
    shuffle = jax.random.permutation(jax.random.fold_in(key, 1000), plan.shape[0])
    return jnp.take(plan, shuffle, axis=0).astype(jnp.int32)


def block_scale(own_key, shape, split, smallest, high):
    gain = 1.0
    for dim, blocks in split:
        draws = jax.random.uniform(jax.random.fold_in(jax.random.fold_in(own_key, 6), dim), (blocks,), jnp.float32, smallest / len(split), high / len(split))
        gain = gain * jnp.repeat(jnp.exp(draws), shape[dim] // blocks).reshape((-1,) + (1,) * (len(shape) - 1 - dim))
    return gain


def scatter_about(rng, extent, deviation, bound, split=(), kind=jnp.bfloat16):
    result = jax.random.normal(rng, extent, jnp.float32) * deviation
    if len(split) > 0:
        result = block_scale(rng, extent, split, -0.22, 0.18) * result
    return jnp.clip(result, min=-bound, max=bound).astype(kind)


def setup_inputs(seed: int = 0) -> dict:
    seeds = jax.random.split(jax.random.key(seed), 9)
    queries = draw_queries(jax.random.fold_in(seeds[8], 71), 0)
    keys = draw_keys(jax.random.fold_in(seeds[8], 71), 0)
    values = draw_values(jax.random.fold_in(seeds[8], 71), 0)
    grad_out = draw_grad_out(jax.random.fold_in(seeds[8], 71), 0)
    out_weight = scatter_about(seeds[4], (D, HD), HD ** -0.5, 0.09375, ((0, 8), (1, 32)))
    tile_plan = draw_tile_plan(jax.random.fold_in(seeds[8], 71), 0)
    row_moment = jnp.clip(jnp.exp(math.log(5.0) - 2.3025851 * jax.random.uniform(seeds[6], (D,), jnp.float32) ** block_scale(seeds[6], (D,), ((0, 8),), -0.2, 0.2)), 0.5, 5.0)
    col_moment = jnp.clip(jnp.exp(math.log(5.0) - 2.3025851 * jax.random.uniform(seeds[7], (HD,), jnp.float32) ** block_scale(seeds[7], (HD,), ((0, 32),), -0.2, 0.2)), 0.5, 5.0)
    return dict(queries=queries, keys=keys, values=values, grad_out=grad_out, out_weight=out_weight, tile_plan=tile_plan, row_moment=row_moment, col_moment=col_moment)


masked_score = -1e+30
moment_decay = 0.9
square_floor = 1e-30

def head_backward(query, key_rows, value, grad, allowed):
    scale = HEAD_DIM ** (-0.5)
    scores = jnp.dot(query, key_rows.T, preferred_element_type=jnp.float32) * scale
    scores = jnp.where(allowed, scores, masked_score)
    top = lax.optimization_barrier(jnp.max(scores, axis=1, keepdims=True))
    total = lax.optimization_barrier(jnp.sum(jnp.where(allowed, jnp.exp(scores - top), 0.0), axis=1, keepdims=True))
    log_norm = top + jnp.log(total)
    probs = jnp.where(allowed, jnp.exp(scores - log_norm), 0.0)
    probs_half = probs.astype(jnp.bfloat16)
    attn_out = jnp.dot(probs_half, value, preferred_element_type=jnp.float32).astype(jnp.bfloat16)
    delta = lax.optimization_barrier(jnp.sum(grad.astype(jnp.float32) * attn_out.astype(jnp.float32), axis=1, keepdims=True))
    dprobs = jnp.dot(grad, value.T, preferred_element_type=jnp.float32)
    dscores = (probs * (dprobs - delta)).astype(jnp.bfloat16)
    value_grad = jnp.dot(probs_half.T, grad, preferred_element_type=jnp.float32)
    query_grad = jnp.dot(dscores, key_rows, preferred_element_type=jnp.float32) * scale
    key_grad = jnp.dot(dscores.T, query, preferred_element_type=jnp.float32) * scale
    return (query_grad.astype(jnp.bfloat16), key_grad.astype(jnp.bfloat16), value_grad.astype(jnp.bfloat16), attn_out)

def split_heads(array):
    return array.reshape(SEQS, LEN, HEADS, HEAD_DIM).transpose(0, 2, 1, 3).reshape(SEQS * HEADS, LEN, HEAD_DIM)

def joined_heads(array):
    return array.reshape(SEQS, HEADS, LEN, HEAD_DIM).transpose(0, 2, 1, 3).reshape(SEQS, LEN, HD)

def reference(queries, keys, values, grad_out, out_weight, tile_plan, row_moment, col_moment):
    blocks = LEN // BLOCK
    codes = (tile_plan[:, 0] * blocks + tile_plan[:, 1]) * blocks + tile_plan[:, 2]
    member = jnp.zeros((SEQS * blocks * blocks,), jnp.int32).at[codes].set(1).reshape(SEQS, blocks, blocks)
    position = jnp.arange(LEN, dtype=jnp.int32)
    causal = position[:, None] >= position[None, :]
    tokens = SEQS * LEN
    attn_grad = jnp.dot(grad_out.reshape(tokens, D), out_weight, preferred_element_type=jnp.float32).astype(jnp.bfloat16)

    def one_head(item):
        query, key_rows, value, grad, index = item
        tiles = lax.dynamic_index_in_dim(member, index // HEADS, 0, keepdims=False)
        wide = jnp.repeat(jnp.repeat(tiles, BLOCK, axis=0), BLOCK, axis=1)
        allowed = (wide > 0) & causal
        return head_backward(query, key_rows, value, grad, allowed)
    results = lax.map(one_head, (split_heads(queries), split_heads(keys), split_heads(values), split_heads(attn_grad.reshape(SEQS, LEN, HD)), jnp.arange(SEQS * HEADS, dtype=jnp.int32)))
    query_grad = joined_heads(results[0])
    key_grad = joined_heads(results[1])
    value_grad = joined_heads(results[2])
    attn_out = joined_heads(results[3])
    weight_grad = lax.dot_general(grad_out.reshape(tokens, D), attn_out.reshape(tokens, HD), (((0,), (0,)), ((), ())), preferred_element_type=jnp.float32)
    squares = weight_grad * weight_grad
    row_square = lax.optimization_barrier(jnp.sum(squares, axis=1)) / HD + square_floor
    col_square = lax.optimization_barrier(jnp.sum(squares, axis=0)) / D + square_floor
    keep = 1.0 - moment_decay
    new_row = moment_decay * row_moment + keep * row_square
    new_col = moment_decay * col_moment + keep * col_square
    moment_mean = jnp.sum(new_row) / D
    update = weight_grad / jnp.sqrt(new_row[:, None] * new_col[None, :] / moment_mean)
    return (query_grad, key_grad, value_grad, update, new_row, new_col)
```

```python
import functools

import jax
import jax.numpy as jnp
from jax import lax
from jax.experimental import pallas as pl
from jax.experimental.pallas import tpu as pltpu
from jax.sharding import PartitionSpec as P

D = 4096
HEAD_DIM = 64
HD = 4096
LEN = 2048
BLOCK = 128
SEQS = 3
ROWS = 8
ZS = 8
XS = 4
SPAN = LEN // ROWS
WIDTH = 128
TOKENS = SEQS * SPAN
UNITS = 6
TILES = LEN // BLOCK
WIDE = 256

masked_score = -1e30
moment_decay = 0.9
square_floor = 1e-30

bf16 = jnp.bfloat16
f32 = jnp.float32
NN = (((1,), (0,)), ((), ()))
NT = (((1,), (1,)), ((), ()))


def dot(a, b, dims=NN):
    return lax.dot_general(a, b, dims, preferred_element_type=f32)


def row_pairs(shift, sources=ROWS, targets=ROWS):
    pairs = [(j, (j + shift) % ROWS) for j in range(ROWS)]
    return [(a, b) for a, b in pairs if a < sources and b < targets]


def z_pairs(shift):
    return [(z * XS + x, (z + shift) % ZS * XS + x) for z in range(ZS) for x in range(XS)]


def x_pairs(shift):
    return [(z * XS + x, z * XS + (x + shift) % XS) for z in range(ZS) for x in range(XS)]


def core_pairs():
    return [(j, j ^ 1) for j in range(ROWS)]


def send_row(a, shift, sources=ROWS, targets=ROWS):
    return lax.ppermute(a, "row", row_pairs(shift, sources, targets))


def send_z(a, shift):
    return lax.ppermute(a, "col", z_pairs(shift))


def send_x(a, shift):
    return lax.ppermute(a, "col", x_pairs(shift))


def aligned(index, size):
    return pl.ds(pl.multiple_of(index * size, size), size)


def call(kernel, outs, args, scratch=(), smem=1, flops=0, us=1.0, limit=16):
    space = lambda i: pltpu.SMEM if i < smem else pltpu.VMEM
    return pl.pallas_call(
        kernel,
        out_shape=[jax.ShapeDtypeStruct(s, t) for s, t in outs],
        in_specs=[pl.BlockSpec(memory_space=space(i)) for i in range(len(args))],
        out_specs=[pl.BlockSpec(memory_space=pltpu.VMEM) for _ in outs],
        scratch_shapes=list(scratch),
        compiler_params=pltpu.CompilerParams(vmem_limit_bytes=limit * 2**20),
        cost_estimate=pl.CostEstimate(
            flops=flops, bytes_accessed=int(us * 3e6), transcendentals=0
        ),
    )(*args)


def unit_of(u):
    u = jnp.minimum(u, UNITS - 1)
    return u // SEQS, u % SEQS


def turn_kernel(at, g, w, ga, gb, w0, w1, w2, w3):
    x = at[2]
    gt = g[...].T
    ga[...] = gt[:HEAD_DIM]
    gb[...] = gt[HEAD_DIM:]
    for s, out in enumerate((w0, w1, w2, w3)):
        out[...] = w[aligned((x + s) % XS, WIDTH), :].T


def pack_kernel(at, plan, q, k, v, *refs):
    outs, (turned, member) = refs[:ROWS], refs[ROWS:]
    r = at[0]
    turned[:WIDTH] = (q[...].astype(f32) * HEAD_DIM ** (-0.5)).astype(bf16).T
    turned[WIDTH : 2 * WIDTH] = k[...].T
    turned[2 * WIDTH :] = v[...].T
    member[...] = jnp.zeros_like(member)
    lane = lax.broadcasted_iota(jnp.int32, (1, WIDE), 1)

    def mark(i, carry):
        row = plan[i, 0] * TILES + plan[i, 2]
        member[pl.ds(row, 1), :] += (lane == plan[i, 1]).astype(f32)
        return carry

    lax.fori_loop(0, plan.shape[0], mark, 0)
    for s, out in enumerate(outs):
        head, seq = unit_of((r + s) % ROWS)
        lanes = aligned(seq, SPAN)
        for part in range(3):
            rows = pl.ds(pl.multiple_of(part * WIDTH + head * HEAD_DIM, HEAD_DIM), HEAD_DIM)
            out[part * HEAD_DIM : (part + 1) * HEAD_DIM] = turned[rows, lanes]
        out[3 * HEAD_DIM :] = member[aligned(seq, TILES), :].astype(bf16)


def weight_kernel(at, w0, w1, w2, w3, out):
    x = at[2]
    for s, piece in enumerate((w0, w1, w2, w3)):
        out[aligned((x + XS - s) % XS, WIDTH), :] = piece[...]


def causal_bias():
    key = lax.broadcasted_iota(jnp.int32, (WIDE, WIDE), 0)
    query = lax.broadcasted_iota(jnp.int32, (WIDE, WIDE), 1)
    return jnp.where(key <= query, 0.0, masked_score).astype(f32)


def biased(score, bias, kb, qb):
    lanes = slice(qb * WIDE, (qb + 1) * WIDE)
    per = WIDE // BLOCK
    parts = []
    for t in range(per):
        row = bias[kb * per + t : kb * per + t + 1, lanes]
        parts.append(score[t * BLOCK : (t + 1) * BLOCK] + row)
    score = jnp.concatenate(parts, axis=0)
    if kb == qb:
        score = score + causal_bias()
    return score


def span_of(b):
    return slice(b * WIDE, (b + 1) * WIDE)


def forward_kernel(at, *refs):
    pieces, refs = refs[:ROWS], refs[ROWS:]
    turned, bias, norm, whole, outs = refs[0], refs[1], refs[2], refs[3], refs[4 : 4 + ROWS]
    kv, qpad, member, scores = refs[4 + ROWS :]
    u = at[0]

    @pl.when(u < UNITS)
    def _():
        member[...] = jnp.zeros_like(member)
        for s, piece in enumerate(pieces):
            turned[:, aligned((u + ROWS - s) % ROWS, SPAN)] = piece[: 3 * HEAD_DIM]
            member[...] += piece[3 * HEAD_DIM :, :BLOCK].astype(f32)
        tile = lax.broadcasted_iota(jnp.int32, (BLOCK, LEN), 0)
        lane = lax.broadcasted_iota(jnp.int32, (BLOCK, LEN), 1) // BLOCK
        spread = jnp.where(tile == lane, 1.0, 0.0).astype(bf16)
        here = dot(member[...].astype(bf16), spread)
        bias[...] = jnp.where(here > 0.5, 0.0, masked_score)
        qpad[:HEAD_DIM] = turned[:HEAD_DIM]
        qpad[HEAD_DIM:] = jnp.zeros((HEAD_DIM, LEN), bf16)
        for b in range(LEN // WIDE):
            kv[span_of(b)] = turned[HEAD_DIM:, span_of(b)].T
        for qb in range(LEN // WIDE):
            qs = span_of(qb)
            query = qpad[:, qs]
            top = jnp.full((1, WIDE), 2 * masked_score, f32)
            for kb in range(qb + 1):
                score = biased(dot(kv[span_of(kb)], query), bias, kb, qb)
                scores[span_of(kb)] = score
                top = jnp.maximum(top, jnp.max(score, axis=0, keepdims=True))
            total = jnp.zeros((1, WIDE), f32)
            acc = jnp.zeros((HEAD_DIM, WIDE), f32)
            for kb in range(qb + 1):
                probs = jnp.exp(scores[span_of(kb)] - top)
                total += jnp.sum(probs, axis=0, keepdims=True)
                acc += dot(turned[2 * HEAD_DIM :, span_of(kb)], probs.astype(bf16))
            whole[:, qs] = (acc / total).astype(bf16)
            norm[:, qs] = jnp.broadcast_to(top + jnp.log(total), (8, WIDE))
        for s, out in enumerate(outs):
            out[...] = whole[:, aligned((u + s) % ROWS, SPAN)]


def gather_kernel(at, *refs):
    pieces, out = refs[:ROWS], refs[ROWS]
    r = at[0]
    for s, piece in enumerate(pieces):
        u = (r + ROWS - s) % ROWS

        @pl.when(u < UNITS)
        def _():
            head, seq = unit_of(u)
            out[aligned(head, HEAD_DIM), aligned(seq, SPAN)] = piece[...]


def project_kernel(at, *refs):
    ws, gs, refs = refs[:ROWS], refs[ROWS : ROWS + 2 * ZS], refs[ROWS + 2 * ZS :]
    allg, own, p1, p2, p3, allw = refs
    r, z, x = at[0], at[1], at[2]
    for k in range(ROWS // 2):
        allw[:, aligned((r + ROWS - 2 * k) % ROWS, WIDTH)] = ws[k][...]
        other = r + 1 - 2 * (r % 2)
        allw[:, aligned((other + ROWS - 2 * k) % ROWS, WIDTH)] = ws[ROWS // 2 + k][...]
    for k in range(ZS):
        for half in range(2):
            block = (z + ZS - k) % ZS * 2 + half
            allg[aligned(block, HEAD_DIM), :] = gs[2 * k + half][...]
    own[...] = dot(allw[aligned(x, WIDTH), :], allg[...])
    for s, out in enumerate((p1, p2, p3)):
        out[...] = dot(allw[aligned((x + s + 1) % XS, WIDTH), :], allg[...]).astype(bf16)


def cotangent_kernel(at, own, p1, p2, p3, *refs):
    outs, whole = refs[:ROWS], refs[ROWS]
    r = at[0]
    total = own[...] + p1[...].astype(f32) + p2[...].astype(f32) + p3[...].astype(f32)
    whole[...] = total.astype(bf16)
    for s, out in enumerate(outs):
        head, seq = unit_of((r + s) % ROWS)
        out[...] = whole[aligned(head, HEAD_DIM), aligned(seq, SPAN)]


def backward_kernel(at, *refs):
    pieces, refs = refs[:ROWS], refs[ROWS:]
    turned, bias, norm, whole, outs = refs[0], refs[1], refs[2], refs[3], refs[4 : 4 + ROWS]
    grad, kv, qpad, gpad, delta, sums, result = refs[4 + ROWS :]
    u = at[0]

    @pl.when(u < UNITS)
    def _():
        for s, piece in enumerate(pieces):
            grad[:, aligned((u + ROWS - s) % ROWS, SPAN)] = piece[...]
        qpad[:HEAD_DIM] = turned[:HEAD_DIM]
        qpad[HEAD_DIM:] = jnp.zeros((HEAD_DIM, LEN), bf16)
        gpad[:HEAD_DIM] = jnp.zeros((HEAD_DIM, LEN), bf16)
        gpad[HEAD_DIM:] = grad[...]
        delta[...] = jnp.broadcast_to(
            jnp.sum(grad[...].astype(f32) * whole[...].astype(f32), axis=0, keepdims=True),
            (8, LEN),
        )
        for b in range(LEN // WIDE):
            kv[span_of(b)] = turned[HEAD_DIM:, span_of(b)].T
        for kb in range(LEN // WIDE):
            ks = span_of(kb)
            key_value = kv[ks]
            key_t = turned[HEAD_DIM : 2 * HEAD_DIM, ks]
            key_acc = jnp.zeros((HEAD_DIM, WIDE), f32)
            value_acc = jnp.zeros((HEAD_DIM, WIDE), f32)
            for qb in range(kb, LEN // WIDE):
                qs = span_of(qb)
                score = biased(dot(key_value, qpad[:, qs]), bias, kb, qb)
                probs = jnp.exp(score - norm[:1, qs])
                dprobs = dot(key_value, gpad[:, qs])
                dscore = (probs * (dprobs - delta[:1, qs])).astype(bf16)
                value_acc += dot(grad[:, qs], probs.astype(bf16), NT)
                key_acc += dot(turned[:HEAD_DIM, qs], dscore, NT)
                part = dot(key_t, dscore)
                if kb == 0:
                    sums[:, qs] = part
                else:
                    sums[:, qs] += part
            result[HEAD_DIM : 2 * HEAD_DIM, ks] = key_acc.astype(bf16)
            result[2 * HEAD_DIM :, ks] = value_acc.astype(bf16)
        result[:HEAD_DIM] = (sums[...] * HEAD_DIM ** (-0.5)).astype(bf16)
        for s, out in enumerate(outs):
            out[...] = result[:, aligned((u + s) % ROWS, SPAN)]


def finish_kernel(at, *refs):
    pieces, outs, whole = refs[:ROWS], refs[ROWS : ROWS + 3], refs[ROWS + 3]
    r = at[0]
    for s, piece in enumerate(pieces):
        u = (r + ROWS - s) % ROWS

        @pl.when(u < UNITS)
        def _():
            head, seq = unit_of(u)
            for part in range(3):
                rows = pl.ds(pl.multiple_of(part * WIDTH + head * HEAD_DIM, HEAD_DIM), HEAD_DIM)
                whole[rows, aligned(seq, SPAN)] = piece[
                    part * HEAD_DIM : (part + 1) * HEAD_DIM, :
                ]

    for part, out in enumerate(outs):
        out[...] = whole[part * WIDTH : (part + 1) * WIDTH].T


def weight_grad_kernel(at, allg, o0, o1, o2, o3, *refs):
    outs, allo, product = refs[:ROWS], refs[ROWS], refs[ROWS + 1]
    r, x = at[0], at[2]
    for s, piece in enumerate((o0, o1, o2, o3)):
        allo[aligned((x + XS - s) % XS, WIDTH), :] = piece[...]
    product[...] = dot(allg[...], allo[...], NT)
    for s, out in enumerate(outs):
        out[...] = product[aligned((r + s) % ROWS, WIDTH), :].astype(out.dtype)


def square_kernel(at, *refs):
    parts, moment, outs, col, whole = refs[:ROWS], refs[8], refs[9:13], refs[13], refs[14]
    x = at[2]
    total = parts[0][...]
    for part in parts[1:]:
        total = total + part[...].astype(f32)
    whole[...] = total
    squares = total * total
    row_sum = lax.dot_general(
        jnp.ones((8, XS * WIDTH), f32),
        squares,
        NT,
        precision=lax.Precision.HIGHEST,
        preferred_element_type=f32,
    )
    col_sum = jnp.sum(squares, axis=0, keepdims=True)
    for s, out in enumerate(outs):
        out[:WIDTH] = whole[:, aligned((x + s) % XS, WIDTH)]
        out[WIDTH:] = row_sum
    col[:, : XS * WIDTH] = jnp.broadcast_to(col_sum, (8, XS * WIDTH))
    everything = jnp.sum(col_sum, axis=1, keepdims=True)
    col[:, XS * WIDTH : (XS + 1) * WIDTH] = jnp.broadcast_to(everything, (8, WIDTH))
    held = jnp.sum(moment[...], axis=1, keepdims=True)
    col[:, (XS + 1) * WIDTH :] = jnp.broadcast_to(held, (8, WIDTH))


def place_kernel(at, *refs):
    cols, parts, refs = refs[:ROWS], refs[ROWS : ROWS + XS], refs[ROWS + XS :]
    grad, rows, outs, held, whole = refs[0], refs[1], refs[2 : 2 + XS], refs[6], refs[7]
    x = at[2]
    for s, part in enumerate(parts):
        source = (x + XS - s) % XS
        grad[aligned(source, WIDTH), :] = part[:WIDTH]
        rows[:, aligned(source, WIDTH)] = part[WIDTH:]
    total = cols[0][...]
    for col in cols[1:]:
        total = total + col[...]
    whole[...] = total
    held[...] = total[:, (XS + 1) * WIDTH :]
    for s, out in enumerate(outs):
        out[:, :WIDTH] = whole[:, aligned((x + s) % XS, WIDTH)]
        out[:, WIDTH:] = whole[:, XS * WIDTH : (XS + 1) * WIDTH]


def moment_kernel(*refs):
    rows, cols, refs = refs[:ZS], refs[ZS : ZS + XS], refs[ZS + XS :]
    row_moment, col_moment, new_row, new_col, everything = refs
    keep = 1.0 - moment_decay
    row = rows[0][...]
    for part in rows[1:]:
        row = row + part[...]
    col = cols[0][...]
    for part in cols[1:]:
        col = col + part[...]
    row_square = row / HD + square_floor
    col_square = col[:, :WIDTH] / D + square_floor
    new_row[...] = moment_decay * row_moment[...] + keep * row_square[:1]
    new_col[...] = moment_decay * col_moment[...] + keep * col_square[:1]
    everything[...] = col[:, WIDTH:]


def update_kernel(*refs):
    totals, (held, grad, new_row, new_col, out) = refs[:ZS], refs[ZS:]
    keep = 1.0 - moment_decay
    total = totals[0][...]
    for part in totals[1:]:
        total = total + part[...]
    row_total = moment_decay * held[...] + keep * (total / HD + D * square_floor)
    mean = row_total[:1] / D
    row = jnp.broadcast_to(new_row[...], (8, new_row.shape[1])).T[:, :1]
    out[...] = grad[...] * lax.rsqrt(row * new_col[...] / mean)


def body(queries, keys, values, grad_out, out_weight, tile_plan, row_moment, col_moment):
    flat = lambda a: a.reshape(TOKENS, WIDTH)
    r, c = lax.axis_index("row"), lax.axis_index("col")
    at = jnp.stack([r, c // XS, c % XS]).astype(jnp.int32)
    rows = range(1, ROWS)
    xs = range(1, XS)

    turned = call(
        turn_kernel,
        [((HEAD_DIM, TOKENS), bf16)] * 2 + [((WIDTH, WIDTH), bf16)] * XS,
        (at, flat(grad_out), out_weight),
    )
    halves, pieces = turned[:2], turned[2:]
    up, down = [list(halves)], [list(halves)]
    for _ in range(ZS // 2 - 1):
        up.append([send_z(a, 1) for a in up[-1]])
        down.append([send_z(a, -1) for a in down[-1]])
    far = [send_z(up[-1][0], 1), send_z(down[-1][1], -1)]
    blocks = up + [far] + down[:0:-1]
    features = [half for block in blocks for half in block]

    packed = call(
        pack_kernel,
        [((3 * HEAD_DIM + TILES, SPAN), bf16)] * ROWS,
        (at, tile_plan, flat(queries), flat(keys), flat(values)),
        scratch=[pltpu.VMEM((3 * WIDTH, TOKENS), bf16), pltpu.VMEM((SEQS * TILES, WIDE), f32)],
        smem=2,
    )
    packed = [packed[0]] + [send_row(packed[s], s, targets=UNITS) for s in rows]

    pieces = [pieces[0]] + [send_x(pieces[s], s) for s in xs]
    (mine,) = call(weight_kernel, [((XS * WIDTH, WIDTH), bf16)], (at, *pieces))
    weights = [mine] + [send_row(mine, 2 * k) for k in range(1, ROWS // 2)]
    weights = weights + [lax.ppermute(w, "row", core_pairs()) for w in weights]

    held = call(
        forward_kernel,
        [
            ((3 * HEAD_DIM, LEN), bf16),
            ((TILES, LEN), f32),
            ((8, LEN), f32),
            ((HEAD_DIM, LEN), bf16),
        ]
        + [((HEAD_DIM, SPAN), bf16)] * ROWS,
        (at, *packed),
        scratch=[
            pltpu.VMEM((LEN, 2 * HEAD_DIM), bf16),
            pltpu.VMEM((2 * HEAD_DIM, LEN), bf16),
            pltpu.VMEM((TILES, BLOCK), f32),
            pltpu.VMEM((LEN, WIDE), f32),
        ],
        us=10.0,
    )
    held, outputs = held[:4], held[4:]

    outputs = [outputs[0]] + [send_row(outputs[s], s, sources=UNITS) for s in rows]
    (attn_out,) = call(gather_kernel, [((WIDTH, TOKENS), bf16)], (at, *outputs))
    attn_outs = [attn_out] + [send_x(attn_out, s) for s in xs]

    allg, *partial = call(
        project_kernel,
        [((ZS * WIDTH, TOKENS), bf16), ((WIDTH, TOKENS), f32)] + [((WIDTH, TOKENS), bf16)] * 3,
        (at, *weights, *features),
        scratch=[pltpu.VMEM((XS * WIDTH, ROWS * WIDTH), bf16)],
        us=4.0,
    )
    partial = [partial[0]] + [send_x(partial[s], s) for s in xs]
    grads = call(
        cotangent_kernel,
        [((HEAD_DIM, SPAN), bf16)] * ROWS,
        (at, *partial),
        scratch=[pltpu.VMEM((WIDTH, TOKENS), bf16)],
    )
    grads = [grads[0]] + [send_row(grads[s], s, targets=UNITS) for s in rows]

    products = call(
        weight_grad_kernel,
        [((WIDTH, XS * WIDTH), f32)] + [((WIDTH, XS * WIDTH), bf16)] * (ROWS - 1),
        (at, allg, *attn_outs),
        scratch=[
            pltpu.VMEM((XS * WIDTH, TOKENS), bf16),
            pltpu.VMEM((ZS * WIDTH, XS * WIDTH), f32),
        ],
        us=4.0,
    )
    products = [products[0]] + [send_row(products[s], s) for s in rows]

    results = call(
        backward_kernel,
        [((3 * HEAD_DIM, SPAN), bf16)] * ROWS,
        (at, *grads, *held),
        scratch=[
            pltpu.VMEM((HEAD_DIM, LEN), bf16),
            pltpu.VMEM((LEN, 2 * HEAD_DIM), bf16),
            pltpu.VMEM((2 * HEAD_DIM, LEN), bf16),
            pltpu.VMEM((2 * HEAD_DIM, LEN), bf16),
            pltpu.VMEM((8, LEN), f32),
            pltpu.VMEM((HEAD_DIM, LEN), f32),
            pltpu.VMEM((3 * HEAD_DIM, LEN), bf16),
        ],
        us=15.0,
    )
    results = [results[0]] + [send_row(results[s], s, sources=UNITS) for s in rows]
    query_grad, key_grad, value_grad = call(
        finish_kernel,
        [((TOKENS, WIDTH), bf16)] * 3,
        (at, *results),
        scratch=[pltpu.VMEM((3 * WIDTH, TOKENS), bf16)],
    )

    row_held = row_moment.reshape(1, -1)
    *squares, col_part = call(
        square_kernel,
        [((WIDTH + 8, WIDTH), f32)] * XS + [((8, (XS + 2) * WIDTH), f32)],
        (at, *products, row_held),
        scratch=[pltpu.VMEM((WIDTH, XS * WIDTH), f32)],
    )
    squares = [squares[0]] + [send_x(squares[s], s) for s in xs]
    col_parts = [col_part] + [send_row(col_part, s) for s in rows]
    weight_grad, row_part, *rest = call(
        place_kernel,
        [((XS * WIDTH, WIDTH), f32), ((8, XS * WIDTH), f32)]
        + [((8, 2 * WIDTH), f32)] * XS
        + [((8, WIDTH), f32)],
        (at, *col_parts, *squares),
        scratch=[pltpu.VMEM((8, (XS + 2) * WIDTH), f32)],
    )
    col_sums, moment_sum = rest[:XS], rest[XS]
    row_parts = [row_part] + [send_z(row_part, s) for s in range(1, ZS)]
    col_sums = [col_sums[0]] + [send_x(col_sums[s], s) for s in xs]
    new_row, new_col, everything = call(
        moment_kernel,
        [((1, XS * WIDTH), f32), ((1, WIDTH), f32), ((8, WIDTH), f32)],
        (*row_parts, *col_sums, row_held, col_moment.reshape(1, -1)),
        smem=0,
    )
    totals = [everything] + [send_z(everything, s) for s in range(1, ZS)]
    (update,) = call(
        update_kernel,
        [((XS * WIDTH, WIDTH), f32)],
        (*totals, moment_sum, weight_grad, new_row, new_col),
        smem=0,
    )
    return (
        query_grad.reshape(queries.shape),
        key_grad.reshape(keys.shape),
        value_grad.reshape(values.shape),
        update,
        new_row.reshape(-1),
        new_col.reshape(-1),
    )


def solution(mesh):
    in_specs = (
        P(None, "row", "col"),
        P(None, "row", "col"),
        P(None, "row", "col"),
        P(None, "row", "col"),
        P("row", "col"),
        P("row", None),
        P("row"),
        P("col"),
    )
    out_specs = (
        P(None, "row", "col"),
        P(None, "row", "col"),
        P(None, "row", "col"),
        P("row", "col"),
        P("row"),
        P("col"),
    )
    return jax.shard_map(body, mesh=mesh, in_specs=in_specs, out_specs=out_specs, check_vma=False)
```

```python
import jax
import jax.numpy as jnp
from jax import lax
from jax.experimental import pallas as pl
from jax.experimental.pallas import tpu as pltpu
from jax.sharding import PartitionSpec as P

D = 4096
HEAD_DIM = 64
HD = 4096
LEN = 2048
BLOCK = 128
SEQS = 3
ROWS = 8
YS = 4
CORES = 2
ZS = 8
XS = 4
SPAN = LEN // ROWS
WIDTH = 128
TOKENS = SEQS * SPAN
PAIR = CORES * SPAN
QKV = 3 * HEAD_DIM
TILES = LEN // BLOCK
WIDE = 256

masked_score = -1e30
moment_decay = 0.9
square_floor = 1e-30

bf16 = jnp.bfloat16
f32 = jnp.float32
NN = (((1,), (0,)), ((), ()))
NT = (((1,), (1,)), ((), ()))
TN = (((0,), (0,)), ((), ()))


def dot(a, b, dims=NN):
    return lax.dot_general(a, b, dims, preferred_element_type=f32)


def y_pairs(shift):
    return [(y * CORES + c, (y + shift) % YS * CORES + c) for y in range(YS) for c in range(CORES)]


def z_pairs(shift):
    return [(z * XS + x, (z + shift) % ZS * XS + x) for z in range(ZS) for x in range(XS)]


def x_pairs(shift):
    return [(z * XS + x, z * XS + (x + shift) % XS) for z in range(ZS) for x in range(XS)]


def send_y(a, shift):
    return lax.ppermute(a, "row", y_pairs(shift))


def send_z(a, shift):
    return lax.ppermute(a, "col", z_pairs(shift))


def send_x(a, shift):
    return lax.ppermute(a, "col", x_pairs(shift))


def swap_core(a):
    return lax.ppermute(a, "row", [(j, j ^ 1) for j in range(ROWS)])


def swap_z(a):
    pairs = [(z * XS + x, (z ^ 1) * XS + x) for z in range(ZS) for x in range(XS)]
    return lax.ppermute(a, "col", pairs)


def aligned(index, size):
    return pl.ds(pl.multiple_of(index * size, size), size)


def call(kernel, outs, args, scratch=(), hbm=0, us=0.0, limit=16):
    spaces = [pltpu.HBM] * hbm
    space = lambda i: spaces[i] if i < len(spaces) else pltpu.VMEM
    return pl.pallas_call(
        kernel,
        out_shape=[jax.ShapeDtypeStruct(s, t) for s, t in outs],
        in_specs=[pl.BlockSpec(memory_space=space(i)) for i in range(len(args))],
        out_specs=[pl.BlockSpec(memory_space=pltpu.VMEM) for _ in outs],
        scratch_shapes=list(scratch),
        compiler_params=pltpu.CompilerParams(vmem_limit_bytes=limit * 2**20),
        cost_estimate=pl.CostEstimate(
            flops=0, bytes_accessed=int(us * 3e6), transcendentals=0
        ),
    )(*args,)


def place():
    row, col = lax.axis_index("row"), lax.axis_index("col")
    return row // CORES, row % CORES, col // XS, col % XS


def seq_of(y):
    return jnp.minimum(y, SEQS - 1)


def pack_kernel(*refs):
    sources, (gt, w0, w1, w2, w3, keep, send) = refs[:6], refs[6:13]
    turned, sem, held = refs[13], refs[14], refs[15:]
    _, core, _, x = place()
    copies = [pltpu.make_async_copy(a, b, sem.at[i]) for i, (a, b) in enumerate(zip(sources, held))]
    for copy in copies:
        copy.start()
    for copy in copies:
        copy.wait()
    g, w, q, k, v, plan = held
    gt[...] = g[...].T
    for s, out in enumerate((w0, w1, w2, w3)):
        out[...] = w[aligned((x + s) % XS, WIDTH), :].T
    turned[:WIDTH] = (q[...].astype(f32) * HEAD_DIM ** (-0.5)).astype(bf16).T
    turned[WIDTH : 2 * WIDTH] = k[...].T
    turned[2 * WIDTH :] = v[...].T
    count = plan.shape[0]
    rows = lax.broadcasted_iota(jnp.int32, (count, SEQS * TILES), 1)
    lanes = lax.broadcasted_iota(jnp.int32, (count, TOKENS), 1)
    here = (plan[:, 0:1] * TILES + plan[:, 2:3] == rows).astype(f32)
    there = (plan[:, 1:2] == lanes).astype(f32)
    member = dot(here.astype(bf16), there.astype(bf16), TN)
    for head, out in ((core, keep), (1 - core, send)):
        for part in range(3):
            rows = pl.ds(pl.multiple_of(part * WIDTH + head * HEAD_DIM, HEAD_DIM), HEAD_DIM)
            out[part * HEAD_DIM : (part + 1) * HEAD_DIM] = turned[rows, :]
        out[QKV:] = member.astype(bf16)


def merge_kernel(keep, got, *outs):
    y, core, _, _ = place()
    for s, out in enumerate(outs):
        seq = seq_of((y + s) % YS)
        out[:QKV, aligned(core, SPAN)] = keep[:QKV, aligned(seq, SPAN)]
        out[:QKV, aligned(1 - core, SPAN)] = got[:QKV, aligned(seq, SPAN)]
        rows = pl.ds(pl.multiple_of(QKV + seq * TILES, TILES), TILES)
        out[QKV:] = keep[rows, :PAIR] + got[rows, :PAIR]


def weight_kernel(w0, w1, w2, w3, out):
    _, _, _, x = place()
    for s, piece in enumerate((w0, w1, w2, w3)):
        out[aligned((x + XS - s) % XS, WIDTH), :] = piece[...]


def causal_bias():
    key = lax.broadcasted_iota(jnp.int32, (WIDE, WIDE), 0)
    query = lax.broadcasted_iota(jnp.int32, (WIDE, WIDE), 1)
    return jnp.where(key <= query, 0.0, masked_score).astype(f32)


def biased(score, bias, kb, qb):
    lanes = slice(qb * WIDE, (qb + 1) * WIDE)
    per = WIDE // BLOCK
    parts = []
    for t in range(per):
        row = bias[kb * per + t : kb * per + t + 1, lanes]
        parts.append(score[t * BLOCK : (t + 1) * BLOCK] + row)
    score = jnp.concatenate(parts, axis=0)
    if kb == qb:
        score = score + causal_bias()
    return score


def span_of(b):
    return slice(b * WIDE, (b + 1) * WIDE)


def forward_kernel(*refs):
    pieces, refs = refs[:YS], refs[YS:]
    turned, bias, norm, whole, outs = refs[0], refs[1], refs[2], refs[3], refs[4 : 4 + YS]
    kv, qpad, member, scores = refs[4 + YS :]
    y, _, _, _ = place()

    @pl.when(y < SEQS)
    def _():
        member[...] = jnp.zeros_like(member)
        for s, piece in enumerate(pieces):
            turned[:, aligned((y + YS - s) % YS, PAIR)] = piece[:QKV]
            member[...] += piece[QKV:, :BLOCK].astype(f32)
        tile = lax.broadcasted_iota(jnp.int32, (BLOCK, LEN), 0)
        lane = lax.broadcasted_iota(jnp.int32, (BLOCK, LEN), 1) // BLOCK
        spread = jnp.where(tile == lane, 1.0, 0.0).astype(bf16)
        here = dot(member[...].astype(bf16), spread)
        bias[...] = jnp.where(here > 0.5, 0.0, masked_score)
        qpad[:HEAD_DIM] = turned[:HEAD_DIM]
        qpad[HEAD_DIM:] = jnp.zeros((HEAD_DIM, LEN), bf16)
        for b in range(LEN // WIDE):
            kv[span_of(b)] = turned[HEAD_DIM:, span_of(b)].T
        for qb in range(LEN // WIDE):
            qs = span_of(qb)
            query = qpad[:, qs]
            top = jnp.full((1, WIDE), 2 * masked_score, f32)
            for kb in range(qb + 1):
                score = biased(dot(kv[span_of(kb)], query), bias, kb, qb)
                scores[span_of(kb)] = score
                top = jnp.maximum(top, jnp.max(score, axis=0, keepdims=True))
            total = jnp.zeros((1, WIDE), f32)
            acc = jnp.zeros((HEAD_DIM, WIDE), f32)
            for kb in range(qb + 1):
                probs = jnp.exp(scores[span_of(kb)] - top)
                total += jnp.sum(probs, axis=0, keepdims=True)
                acc += dot(turned[2 * HEAD_DIM :, span_of(kb)], probs.astype(bf16))
            whole[:, qs] = (acc / total).astype(bf16)
            norm[:, qs] = jnp.broadcast_to(top + jnp.log(total), (8, WIDE))
        for s, out in enumerate(outs):
            out[...] = whole[:, aligned((y + s) % YS, PAIR)]


def gather_kernel(*refs):
    pieces, out = refs[:YS], refs[YS]
    y, _, _, _ = place()
    for s, piece in enumerate(pieces):
        source = (y + YS - s) % YS

        @pl.when(source < SEQS)
        def _():
            seq = seq_of(source)
            for core in range(CORES):
                lanes = pl.ds(pl.multiple_of(core * TOKENS + seq * SPAN, SPAN), SPAN)
                out[:, lanes] = piece[:, core * SPAN : (core + 1) * SPAN]


def project_kernel(*refs):
    ws, gs, refs = refs[:ROWS], refs[ROWS : ROWS + ZS], refs[ROWS + ZS :]
    allg, own, p1, p2, p3, allw = refs
    y, core, z, x = place()
    for k in range(YS):
        for c in range(CORES):
            other = core + c - 2 * core * c
            source = (y + YS - k) % YS * CORES + other
            allw[:, aligned(source, WIDTH)] = ws[c * YS + k][...]
    for k in range(ZS):
        allg[aligned((z + ZS - k) % ZS, WIDTH), :] = gs[k][...]
    own[...] = dot(allw[aligned(x, WIDTH), :], allg[...])
    for s, out in enumerate((p1, p2, p3)):
        out[...] = dot(allw[aligned((x + s + 1) % XS, WIDTH), :], allg[...]).astype(bf16)


def cotangent_kernel(own, p1, p2, p3, keep, send, whole):
    _, core, _, _ = place()
    total = own[...] + p1[...].astype(f32) + p2[...].astype(f32) + p3[...].astype(f32)
    whole[...] = total.astype(bf16)
    keep[...] = whole[aligned(core, HEAD_DIM), :]
    send[...] = whole[aligned(1 - core, HEAD_DIM), :]


def spread_kernel(keep, got, *outs):
    y, core, _, _ = place()
    for s, out in enumerate(outs):
        seq = seq_of((y + s) % YS)
        out[:, aligned(core, SPAN)] = keep[:, aligned(seq, SPAN)]
        out[:, aligned(1 - core, SPAN)] = got[:, aligned(seq, SPAN)]


def backward_kernel(*refs):
    pieces, refs = refs[:YS], refs[YS:]
    turned, bias, norm, whole, outs = refs[0], refs[1], refs[2], refs[3], refs[4 : 4 + YS]
    grad, kv, qpad, gpad, delta, sums, result = refs[4 + YS :]
    y, _, _, _ = place()

    @pl.when(y < SEQS)
    def _():
        for s, piece in enumerate(pieces):
            grad[:, aligned((y + YS - s) % YS, PAIR)] = piece[...]
        qpad[:HEAD_DIM] = turned[:HEAD_DIM]
        qpad[HEAD_DIM:] = jnp.zeros((HEAD_DIM, LEN), bf16)
        gpad[:HEAD_DIM] = jnp.zeros((HEAD_DIM, LEN), bf16)
        gpad[HEAD_DIM:] = grad[...]
        delta[...] = jnp.broadcast_to(
            jnp.sum(grad[...].astype(f32) * whole[...].astype(f32), axis=0, keepdims=True),
            (8, LEN),
        )
        for b in range(LEN // WIDE):
            kv[span_of(b)] = turned[HEAD_DIM:, span_of(b)].T
        for kb in range(LEN // WIDE):
            ks = span_of(kb)
            key_value = kv[ks]
            key_t = turned[HEAD_DIM : 2 * HEAD_DIM, ks]
            key_acc = jnp.zeros((HEAD_DIM, WIDE), f32)
            value_acc = jnp.zeros((HEAD_DIM, WIDE), f32)
            for qb in range(kb, LEN // WIDE):
                qs = span_of(qb)
                score = biased(dot(key_value, qpad[:, qs]), bias, kb, qb)
                probs = jnp.exp(score - norm[:1, qs])
                dprobs = dot(key_value, gpad[:, qs])
                dscore = (probs * (dprobs - delta[:1, qs])).astype(bf16)
                value_acc += dot(grad[:, qs], probs.astype(bf16), NT)
                key_acc += dot(turned[:HEAD_DIM, qs], dscore, NT)
                part = dot(key_t, dscore)
                if kb == 0:
                    sums[:, qs] = part
                else:
                    sums[:, qs] += part
            result[HEAD_DIM : 2 * HEAD_DIM, ks] = key_acc.astype(bf16)
            result[2 * HEAD_DIM :, ks] = value_acc.astype(bf16)
        result[:HEAD_DIM] = (sums[...] * HEAD_DIM ** (-0.5)).astype(bf16)
        for s, out in enumerate(outs):
            out[...] = result[:, aligned((y + s) % YS, PAIR)]


def join_kernel(*refs):
    pieces, col, outs = refs[:YS], refs[YS], refs[YS + 1 :]
    value = col[:1, :]
    high = value.astype(bf16)
    rest = value - high.astype(f32)
    middle = rest.astype(bf16)
    low = (rest - middle.astype(f32)).astype(bf16)
    for piece, out in zip(pieces, outs):
        out[:QKV] = piece[...]
        out[QKV:] = jnp.zeros((TILES, PAIR), bf16)
        for i, term in enumerate((high, middle, low)):
            out[QKV + i : QKV + i + 1, : 3 * WIDTH] = term


def collect_kernel(*refs):
    pieces, keep, send, col = refs[:YS], refs[YS], refs[YS + 1], refs[YS + 2]
    y, core, _, _ = place()
    total = jnp.zeros((1, 3 * WIDTH), f32)
    for s, piece in enumerate(pieces):
        source = (y + YS - s) % YS
        terms = piece[QKV:, : 3 * WIDTH].astype(f32)
        total = total + (terms[2:3] + terms[1:2] + terms[:1])

        @pl.when(source < SEQS)
        def _():
            lanes = aligned(seq_of(source), SPAN)
            keep[:, lanes] = piece[:QKV, aligned(core, SPAN)]
            send[:, lanes] = piece[:QKV, aligned(1 - core, SPAN)]

    col[...] = jnp.broadcast_to(total, (8, 3 * WIDTH))


def finish_kernel(keep, got, q, k, v, whole):
    _, core, _, _ = place()
    for part, out in enumerate((q, k, v)):
        rows = slice(part * HEAD_DIM, (part + 1) * HEAD_DIM)
        whole[part, aligned(core, HEAD_DIM), :] = keep[rows, :]
        whole[part, aligned(1 - core, HEAD_DIM), :] = got[rows, :]
        out[...] = whole[part].T


def weight_grad_kernel(mine, theirs, o0, o1, o2, o3, *refs):
    outs, allg, allo, product = refs[:YS], refs[YS], refs[YS + 1], refs[YS + 2]
    y, core, _, x = place()
    for s, piece in enumerate((o0, o1, o2, o3)):
        allo[aligned((x + XS - s) % XS, HEAD_DIM), :] = piece[...]
    allg[:, aligned(core, TOKENS)] = mine[...]
    allg[:, aligned(1 - core, TOKENS)] = theirs[...]
    product[...] = dot(allg[...], allo[...], NT)
    for s, out in enumerate(outs):
        out[...] = product[aligned((y + s) % YS, CORES * WIDTH), :].astype(out.dtype)


def total_kernel(*refs):
    parts, (keep, send, whole) = refs[:YS], refs[YS:]
    _, core, _, _ = place()
    total = parts[0][...]
    for part in parts[1:]:
        total = total + part[...].astype(f32)
    whole[...] = total
    square = jnp.sum(jnp.sum(total * total, axis=0, keepdims=True), axis=1, keepdims=True)
    for half, out in ((core, keep), (1 - core, send)):
        out[:WIDTH] = whole[aligned(half, WIDTH), :]
        out[WIDTH:] = jnp.broadcast_to(square, (8, XS * HEAD_DIM))


def square_kernel(keep, got, *refs):
    outs, whole = refs[:XS], refs[XS]
    _, core, _, x = place()
    first = core == 0
    for block in range(XS):
        cols = slice(block * HEAD_DIM, (block + 1) * HEAD_DIM)
        a, b = keep[:WIDTH, cols], got[:WIDTH, cols]
        low, high = jnp.where(first, a, b), jnp.where(first, b, a)
        whole[:, block * WIDTH : (block + 1) * WIDTH] = jnp.concatenate([low, high], axis=1)
    values = whole[...]
    row_sum = lax.dot_general(
        jnp.ones((8, XS * WIDTH), f32),
        values * values,
        NT,
        precision=lax.Precision.HIGHEST,
        preferred_element_type=f32,
    )
    square = keep[WIDTH:, :WIDTH] + got[WIDTH:, :WIDTH]
    for s, out in enumerate(outs):
        out[:WIDTH] = whole[:, aligned((x + s) % XS, WIDTH)]
        out[WIDTH : WIDTH + 8] = row_sum
        out[WIDTH + 8 :] = square


def place_kernel(*refs):
    parts, (moment, grad, rows, cols) = refs[:XS], refs[XS:]
    _, _, _, x = place()
    square = jnp.zeros((8, WIDTH), f32)
    col = jnp.zeros((1, WIDTH), f32)
    for s, part in enumerate(parts):
        source = (x + XS - s) % XS
        values = part[:WIDTH]
        grad[aligned(source, WIDTH), :] = values
        rows[:, aligned(source, WIDTH)] = part[WIDTH : WIDTH + 8]
        square = square + part[WIDTH + 8 :]
        col = col + jnp.sum(values * values, axis=0, keepdims=True)
    rows[:, XS * WIDTH :] = square
    cols[:, :WIDTH] = jnp.broadcast_to(col, (8, WIDTH))
    held = jnp.sum(moment[...], axis=1, keepdims=True)
    cols[:, WIDTH:] = jnp.broadcast_to(held, (8, WIDTH))


def reduce_kernel(r0, r1, r2, r3, c0, c1, rows, cols):
    row = r0[...] + r1[...] + r2[...] + r3[...]
    rows[...] = row[:, : XS * WIDTH]
    cols[:, : 2 * WIDTH] = c0[...] + c1[...]
    cols[:, 2 * WIDTH :] = row[:, XS * WIDTH :]


def update_kernel(col, rows, grad, row_moment, col_moment, out, new_row, new_col):
    keep = 1.0 - moment_decay
    row_square = rows[:1] / HD + square_floor
    col_square = col[:1, :WIDTH] / D + square_floor
    new_row[...] = moment_decay * row_moment[...] + keep * row_square
    new_col[...] = moment_decay * col_moment[...] + keep * col_square
    held, total = col[:1, WIDTH : 2 * WIDTH], col[:1, 2 * WIDTH :]
    mean = (moment_decay * held + keep * (total / HD + D * square_floor)) / D
    row = jnp.broadcast_to(new_row[...], (8, new_row.shape[1])).T[:, :1]
    out[...] = grad[...] * lax.rsqrt(row * new_col[...] / mean)


def together(arrays):
    return list(lax.optimization_barrier(tuple(arrays)))


def after(arrays, first):
    return together([*arrays, first])[:-1]


def body(queries, keys, values, grad_out, out_weight, tile_plan, row_moment, col_moment):
    flat = lambda a: a.reshape(TOKENS, WIDTH)
    ys = range(1, YS)
    xs = range(1, XS)

    turned, *pieces, keep, send = call(
        pack_kernel,
        [((WIDTH, TOKENS), bf16)]
        + [((WIDTH, WIDTH), bf16)] * XS
        + [((QKV + SEQS * TILES, TOKENS), bf16)] * 2,
        (flat(grad_out), out_weight, flat(queries), flat(keys), flat(values), tile_plan),
        scratch=[
            pltpu.VMEM((3 * WIDTH, TOKENS), bf16),
            pltpu.SemaphoreType.DMA((6,)),
            pltpu.VMEM((TOKENS, WIDTH), bf16),
            pltpu.VMEM((XS * WIDTH, WIDTH), bf16),
        ]
        + [pltpu.VMEM((TOKENS, WIDTH), bf16)] * 3
        + [pltpu.VMEM(tile_plan.shape, jnp.int32)],
        hbm=6,
        limit=62,
    )

    pieces = [pieces[0]] + [send_x(pieces[s], s) for s in xs]
    got = swap_core(send)
    packed = call(merge_kernel, [((QKV + TILES, PAIR), bf16)] * YS, (keep, got))
    (mine,) = call(weight_kernel, [((XS * WIDTH, WIDTH), bf16)], (*pieces,))

    turned, *packed = together([turned, *packed])
    up, down = [turned, send_z(turned, 1)], [turned, send_z(turned, -1)]
    packed = after(packed, mine)
    packed = [packed[0]] + [send_y(packed[s], s) for s in ys]
    up.append(send_z(up[1], 1))
    down.append(send_z(down[1], -1))
    mine, up[2], down[2], *packed = together([mine, up[2], down[2], *packed])
    weights = [mine] + [send_y(mine, s) for s in ys]
    up.append(send_z(up[2], 1))
    down.append(send_z(down[2], -1))

    held = call(
        forward_kernel,
        [((QKV, LEN), bf16), ((TILES, LEN), f32), ((8, LEN), f32), ((HEAD_DIM, LEN), bf16)]
        + [((HEAD_DIM, PAIR), bf16)] * YS,
        (*packed,),
        scratch=[
            pltpu.VMEM((LEN, 2 * HEAD_DIM), bf16),
            pltpu.VMEM((2 * HEAD_DIM, LEN), bf16),
            pltpu.VMEM((TILES, BLOCK), f32),
            pltpu.VMEM((LEN, WIDE), f32),
        ],
        us=6.0,
    )
    weights = after(weights, held[0])
    up[3] = after([up[3]], held[0])[0]
    features = up + [send_z(up[3], 1)] + down[:0:-1]
    weights = weights + [swap_core(w) for w in weights]
    held, outputs = held[:4], held[4:]

    outputs = [outputs[0]] + [send_y(outputs[s], s) for s in ys]
    (attn_out,) = call(gather_kernel, [((HEAD_DIM, CORES * TOKENS), bf16)], (*outputs,))
    *weights, attn_out = together([*weights, attn_out])
    attn_outs = [attn_out] + [send_x(attn_out, s) for s in xs]

    allg, *partial = call(
        project_kernel,
        [((ZS * WIDTH, TOKENS), bf16), ((WIDTH, TOKENS), f32)] + [((WIDTH, TOKENS), bf16)] * 3,
        (*weights, *features),
        scratch=[pltpu.VMEM((XS * WIDTH, ROWS * WIDTH), bf16)],
    )
    theirs = swap_core(allg)
    partial = [partial[0]] + [send_x(partial[s], s) for s in xs]
    keep, send = call(
        cotangent_kernel,
        [((HEAD_DIM, TOKENS), bf16)] * 2,
        (*partial,),
        scratch=[pltpu.VMEM((WIDTH, TOKENS), bf16)],
    )
    grads = call(spread_kernel, [((HEAD_DIM, PAIR), bf16)] * YS, (keep, swap_core(send)))
    grads = [grads[0]] + [send_y(grads[s], s) for s in ys]

    block = (CORES * WIDTH, XS * HEAD_DIM)
    products = call(
        weight_grad_kernel,
        [(block, f32)] + [(block, bf16)] * (YS - 1),
        (allg, theirs, *attn_outs),
        scratch=[
            pltpu.VMEM((ZS * WIDTH, CORES * TOKENS), bf16),
            pltpu.VMEM((XS * HEAD_DIM, CORES * TOKENS), bf16),
            pltpu.VMEM((ZS * WIDTH, XS * HEAD_DIM), f32),
        ],
        limit=24,
    )
    products = [products[0]] + [send_y(products[s], s) for s in ys]
    keep, send = call(
        total_kernel,
        [((WIDTH + 8, XS * HEAD_DIM), f32)] * 2,
        (*products,),
        scratch=[pltpu.VMEM(block, f32)],
    )
    squares = call(
        square_kernel,
        [((WIDTH + 16, WIDTH), f32)] * XS,
        (keep, swap_core(send)),
        scratch=[pltpu.VMEM((WIDTH, XS * WIDTH), f32)],
    )
    squares = [squares[0]] + [send_x(squares[s], s) for s in xs]
    row_held = row_moment.reshape(1, -1)
    weight_grad, row_part, col_part = call(
        place_kernel,
        [((XS * WIDTH, WIDTH), f32), ((8, (XS + 1) * WIDTH), f32), ((8, 2 * WIDTH), f32)],
        (*squares, row_held),
    )

    row_part = row_part + swap_z(row_part)
    grads = after(grads, row_part)
    row_parts = [row_part] + [send_z(row_part, s) for s in (2, 4, 6)]
    results = call(
        backward_kernel,
        [((QKV, PAIR), bf16)] * YS,
        (*grads, *held),
        scratch=[
            pltpu.VMEM((HEAD_DIM, LEN), bf16),
            pltpu.VMEM((LEN, 2 * HEAD_DIM), bf16),
            pltpu.VMEM((2 * HEAD_DIM, LEN), bf16),
            pltpu.VMEM((2 * HEAD_DIM, LEN), bf16),
            pltpu.VMEM((8, LEN), f32),
            pltpu.VMEM((HEAD_DIM, LEN), f32),
            pltpu.VMEM((QKV, LEN), bf16),
        ],
        us=10.0,
    )
    row_sum, col_part = call(
        reduce_kernel,
        [((8, XS * WIDTH), f32), ((8, 3 * WIDTH), f32)],
        (*row_parts, col_part, swap_core(col_part)),
    )
    results = call(
        join_kernel, [((QKV + TILES, PAIR), bf16)] * YS, (*results, col_part)
    )
    results = [results[0]] + [send_y(results[s], s) for s in ys]
    keep, send, col_sum = call(
        collect_kernel,
        [((QKV, TOKENS), bf16)] * 2 + [((8, 3 * WIDTH), f32)],
        (*results,),
    )
    query_grad, key_grad, value_grad = call(
        finish_kernel,
        [((TOKENS, WIDTH), bf16)] * 3,
        (keep, swap_core(send)),
        scratch=[pltpu.VMEM((3, WIDTH, TOKENS), bf16)],
    )

    update, new_row, new_col = call(
        update_kernel,
        [((XS * WIDTH, WIDTH), f32), ((1, XS * WIDTH), f32), ((1, WIDTH), f32)],
        (col_sum, row_sum, weight_grad, row_held, col_moment.reshape(1, -1)),
    )
    return (
        query_grad.reshape(queries.shape),
        key_grad.reshape(keys.shape),
        value_grad.reshape(values.shape),
        update,
        new_row.reshape(-1),
        new_col.reshape(-1),
    )


def solution(mesh):
    in_specs = (
        P(None, "row", "col"),
        P(None, "row", "col"),
        P(None, "row", "col"),
        P(None, "row", "col"),
        P("row", "col"),
        P("row", None),
        P("row"),
        P("col"),
    )
    out_specs = (
        P(None, "row", "col"),
        P(None, "row", "col"),
        P(None, "row", "col"),
        P("row", "col"),
        P("row"),
        P("col"),
    )
    return jax.shard_map(body, mesh=mesh, in_specs=in_specs, out_specs=out_specs, check_vma=False)
```

```python
import jax
import jax.numpy as jnp
from jax import lax
from jax.experimental import pallas as pl
from jax.experimental.pallas import tpu as pltpu
from jax.sharding import PartitionSpec as P

D = 4096
HEAD_DIM = 64
HD = 4096
LEN = 2048
BLOCK = 128
SEQS = 3
ROWS = 8
YS = 4
CORES = 2
ZS = 8
XS = 4
SPAN = LEN // ROWS
WIDTH = 128
TOKENS = SEQS * SPAN
PAIR = CORES * SPAN
QKV = 3 * HEAD_DIM
TILES = LEN // BLOCK
WIDE = 256
KEYS = (range(0, 2), range(2, 4), range(4, 8))

masked_score = -1e30
moment_decay = 0.9
square_floor = 1e-30

bf16 = jnp.bfloat16
f32 = jnp.float32
NN = (((1,), (0,)), ((), ()))
NT = (((1,), (1,)), ((), ()))


def dot(a, b, dims=NN):
    return lax.dot_general(a, b, dims, preferred_element_type=f32)


def y_pairs(shift):
    return [(y * CORES + c, (y + shift) % YS * CORES + c) for y in range(YS) for c in range(CORES)]


def z_pairs(shift):
    return [(z * XS + x, (z + shift) % ZS * XS + x) for z in range(ZS) for x in range(XS)]


def x_pairs(shift):
    return [(z * XS + x, z * XS + (x + shift) % XS) for z in range(ZS) for x in range(XS)]


def send_y(a, shift):
    return lax.ppermute(a, "row", y_pairs(shift))


def send_z(a, shift):
    return lax.ppermute(a, "col", z_pairs(shift))


def send_x(a, shift):
    return lax.ppermute(a, "col", x_pairs(shift))


def swap_core(a):
    return lax.ppermute(a, "row", [(j, j ^ 1) for j in range(ROWS)])


def swap_z(a, bit):
    pairs = [(z * XS + x, (z ^ bit) * XS + x) for z in range(ZS) for x in range(XS)]
    return lax.ppermute(a, "col", pairs)


def aligned(index, size):
    return pl.ds(pl.multiple_of(index * size, size), size)


def call(kernel, outs, args, scratch=(), hbm=0, us=0.5, limit=16):
    spaces = [pltpu.HBM] * hbm
    space = lambda i: spaces[i] if i < len(spaces) else pltpu.VMEM
    return pl.pallas_call(
        kernel,
        out_shape=[jax.ShapeDtypeStruct(s, t) for s, t in outs],
        in_specs=[pl.BlockSpec(memory_space=space(i)) for i in range(len(args))],
        out_specs=[pl.BlockSpec(memory_space=pltpu.VMEM) for _ in outs],
        scratch_shapes=list(scratch),
        compiler_params=pltpu.CompilerParams(vmem_limit_bytes=limit * 2**20),
        cost_estimate=pl.CostEstimate(
            flops=int(us * 1.1e9), bytes_accessed=int(us * 3e6), transcendentals=0
        ),
    )(*args,)


def place():
    row, col = lax.axis_index("row"), lax.axis_index("col")
    return row // CORES, row % CORES, col // XS, col % XS


def seq_of(y):
    return jnp.minimum(y, SEQS - 1)


def pack_kernel(*refs):
    sources, (gt, w0, w1, w2, w3, keep, send) = refs[:6], refs[6:13]
    turned, sem, held = refs[13], refs[14], refs[15:]
    _, core, _, x = place()
    copies = [pltpu.make_async_copy(a, b, sem.at[i]) for i, (a, b) in enumerate(zip(sources, held))]
    for copy in copies:
        copy.start()
    for copy in copies:
        copy.wait()
    g, w, q, k, v, plan = held
    gt[...] = g[...].T
    for s, out in enumerate((w0, w1, w2, w3)):
        out[...] = w[aligned((x + s) % XS, WIDTH), :].T
    turned[:WIDTH] = (q[...].astype(f32) * HEAD_DIM ** (-0.5)).astype(bf16).T
    turned[WIDTH : 2 * WIDTH] = k[...].T
    turned[2 * WIDTH :] = v[...].T
    count = plan.shape[1]
    rows = lax.broadcasted_iota(jnp.int32, (SEQS * TILES, count), 0)
    lanes = lax.broadcasted_iota(jnp.int32, (WIDTH, count), 0)
    here = (plan[0:1, :] * TILES + plan[2:3, :] == rows).astype(f32)
    there = (plan[1:2, :] == lanes).astype(f32)
    member = dot(here.astype(bf16), there.astype(bf16), NT)
    for head, out in ((core, keep), (1 - core, send)):
        for part in range(3):
            rows = pl.ds(pl.multiple_of(part * WIDTH + head * HEAD_DIM, HEAD_DIM), HEAD_DIM)
            out[part * HEAD_DIM : (part + 1) * HEAD_DIM] = turned[rows, :]
        out[QKV:, :WIDTH] = member.astype(bf16)


def merge_kernel(keep, got, *outs):
    y, core, _, _ = place()
    for s, out in enumerate(outs):
        seq = seq_of((y + s) % YS)
        out[:QKV, aligned(core, SPAN)] = keep[:QKV, aligned(seq, SPAN)]
        out[:QKV, aligned(1 - core, SPAN)] = got[:QKV, aligned(seq, SPAN)]
        rows = pl.ds(pl.multiple_of(QKV + seq * TILES, TILES), TILES)
        out[QKV:, :WIDTH] = keep[rows, :WIDTH] + got[rows, :WIDTH]


def causal_bias():
    key = lax.broadcasted_iota(jnp.int32, (WIDE, WIDE), 0)
    query = lax.broadcasted_iota(jnp.int32, (WIDE, WIDE), 1)
    return jnp.where(key <= query, 0.0, masked_score).astype(f32)


def biased(score, bias, kb, qb):
    lanes = slice(qb * WIDE, (qb + 1) * WIDE)
    per = WIDE // BLOCK
    parts = []
    for t in range(per):
        row = bias[kb * per + t : kb * per + t + 1, lanes]
        parts.append(score[t * BLOCK : (t + 1) * BLOCK] + row)
    score = jnp.concatenate(parts, axis=0)
    if kb == qb:
        score = score + causal_bias()
    return score


def span_of(b):
    return slice(b * WIDE, (b + 1) * WIDE)


def forward_kernel(*refs):
    pieces, refs = refs[:YS], refs[YS:]
    turned, bias, norm, whole, kv, outs = *refs[:5], refs[5 : 5 + YS]
    qpad, member, scores = refs[5 + YS :]
    y, _, _, _ = place()

    @pl.when(y < SEQS)
    def _():
        member[...] = jnp.zeros_like(member)
        for s, piece in enumerate(pieces):
            turned[:, aligned((y + YS - s) % YS, PAIR)] = piece[:QKV]
            member[...] += piece[QKV:, :BLOCK].astype(f32)
        tile = lax.broadcasted_iota(jnp.int32, (BLOCK, LEN), 0)
        lane = lax.broadcasted_iota(jnp.int32, (BLOCK, LEN), 1) // BLOCK
        spread = jnp.where(tile == lane, 1.0, 0.0).astype(bf16)
        here = dot(member[...].astype(bf16), spread)
        bias[...] = jnp.where(here > 0.5, 0.0, masked_score)
        qpad[:HEAD_DIM] = turned[:HEAD_DIM]
        qpad[HEAD_DIM:] = jnp.zeros((HEAD_DIM, LEN), bf16)
        for b in range(LEN // WIDE):
            kv[span_of(b)] = turned[HEAD_DIM:, span_of(b)].T
        for qb in range(LEN // WIDE):
            qs = span_of(qb)
            query = qpad[:, qs]
            top = jnp.full((1, WIDE), 2 * masked_score, f32)
            for kb in range(qb + 1):
                score = biased(dot(kv[span_of(kb)], query), bias, kb, qb)
                scores[span_of(kb)] = score
                top = jnp.maximum(top, jnp.max(score, axis=0, keepdims=True))
            total = jnp.zeros((1, WIDE), f32)
            acc = jnp.zeros((HEAD_DIM, WIDE), f32)
            for kb in range(qb + 1):
                probs = jnp.exp(scores[span_of(kb)] - top)
                total += jnp.sum(probs, axis=0, keepdims=True)
                acc += dot(turned[2 * HEAD_DIM :, span_of(kb)], probs.astype(bf16))
            whole[:, qs] = (acc / total).astype(bf16)
            norm[:, qs] = jnp.broadcast_to(top + jnp.log(total), (8, WIDE))
        for s, out in enumerate(outs):
            out[...] = whole[:, aligned((y + s) % YS, PAIR)]


def join_kernel(*refs):
    pieces, blocks, outs = refs[:YS], refs[YS : YS + XS], refs[YS + XS :]
    _, _, _, x = place()
    for piece, out in zip(pieces, outs):
        out[:HEAD_DIM] = piece[...]
        for s, block in enumerate(blocks):
            out[HEAD_DIM:, aligned((x + XS - s) % XS, WIDTH)] = block[...]


def gather_kernel(*refs):
    pieces, out, weight = refs[:YS], refs[YS], refs[YS + 1]
    y, _, _, _ = place()
    for s, piece in enumerate(pieces):
        source = (y + YS - s) % YS
        for block in range(XS):
            cols = slice(block * WIDTH, (block + 1) * WIDTH)
            weight[cols, aligned(source, WIDTH)] = piece[HEAD_DIM:, cols]

        @pl.when(source < SEQS)
        def _():
            seq = seq_of(source)
            for core in range(CORES):
                lanes = pl.ds(pl.multiple_of(core * TOKENS + seq * SPAN, SPAN), SPAN)
                out[:, lanes] = piece[:HEAD_DIM, core * SPAN : (core + 1) * SPAN]


def project_kernel(mine, theirs, *refs):
    gs, (allg, own, p1, p2, p3, allw) = refs[:ZS], refs[ZS:]
    _, core, z, x = place()
    for k in range(YS):
        cols = slice(k * WIDTH, (k + 1) * WIDTH)
        allw[:, aligned(k * CORES + core, WIDTH)] = mine[:, cols]
        allw[:, aligned(k * CORES + 1 - core, WIDTH)] = theirs[:, cols]
    for k in range(ZS):
        allg[aligned((z + ZS - k) % ZS, WIDTH), :] = gs[k][...]
    own[...] = dot(allw[aligned(x, WIDTH), :], allg[...])
    for s, out in enumerate((p1, p2, p3)):
        out[...] = dot(allw[aligned((x + s + 1) % XS, WIDTH), :], allg[...]).astype(bf16)


def cotangent_kernel(own, p1, p2, p3, keep, send, whole):
    _, core, _, _ = place()
    total = own[...] + p1[...].astype(f32) + p2[...].astype(f32) + p3[...].astype(f32)
    whole[...] = total.astype(bf16)
    keep[...] = whole[aligned(core, HEAD_DIM), :]
    send[...] = whole[aligned(1 - core, HEAD_DIM), :]


def spread_kernel(keep, got, *outs):
    y, core, _, _ = place()
    for s, out in enumerate(outs):
        seq = seq_of((y + s) % YS)
        out[:, aligned(core, SPAN)] = keep[:, aligned(seq, SPAN)]
        out[:, aligned(1 - core, SPAN)] = got[:, aligned(seq, SPAN)]


def backward_blocks(blocks, turned, bias, norm, kv, qpad, gpad, delta, sums, result):
    for kb in blocks:
        ks = span_of(kb)
        here = slice((kb - blocks[0]) * WIDE, (kb - blocks[0] + 1) * WIDE)
        key_value = kv[ks]
        key_t = turned[HEAD_DIM : 2 * HEAD_DIM, ks]
        key_acc = jnp.zeros((HEAD_DIM, WIDE), f32)
        value_acc = jnp.zeros((HEAD_DIM, WIDE), f32)
        for qb in range(kb, LEN // WIDE):
            qs = span_of(qb)
            score = biased(dot(key_value, qpad[:, qs]), bias, kb, qb)
            probs = jnp.exp(score - norm[:1, qs])
            dprobs = dot(key_value, gpad[:, qs])
            dscore = (probs * (dprobs - delta[:1, qs])).astype(bf16)
            value_acc += dot(gpad[HEAD_DIM:, qs], probs.astype(bf16), NT)
            key_acc += dot(turned[:HEAD_DIM, qs], dscore, NT)
            part = dot(key_t, dscore)
            if kb == 0:
                sums[:, qs] = part
            else:
                sums[:, qs] += part
        result[:HEAD_DIM, here] = key_acc.astype(bf16)
        result[HEAD_DIM:, here] = value_acc.astype(bf16)


def first_backward_kernel(*refs):
    pieces, (turned, bias, norm, whole, kv) = refs[:YS], refs[YS : YS + 5]
    qpad, gpad, delta, sums, result = refs[YS + 5 :]
    y, _, _, _ = place()

    @pl.when(y < SEQS)
    def _():
        qpad[:HEAD_DIM] = turned[:HEAD_DIM]
        qpad[HEAD_DIM:] = jnp.zeros((HEAD_DIM, LEN), bf16)
        gpad[:HEAD_DIM] = jnp.zeros((HEAD_DIM, LEN), bf16)
        for s, piece in enumerate(pieces):
            gpad[HEAD_DIM:, aligned((y + YS - s) % YS, PAIR)] = piece[...]
        products = gpad[HEAD_DIM:].astype(f32) * whole[...].astype(f32)
        delta[...] = jnp.broadcast_to(jnp.sum(products, axis=0, keepdims=True), (8, LEN))
        backward_blocks(KEYS[0], turned, bias, norm, kv, qpad, gpad, delta, sums, result)


def second_backward_kernel(turned, bias, norm, kv, qpad, gpad, delta, before, sums, result):
    y, _, _, _ = place()

    @pl.when(y < SEQS)
    def _():
        sums[...] = before[...]
        backward_blocks(KEYS[1], turned, bias, norm, kv, qpad, gpad, delta, sums, result)


def last_backward_kernel(turned, bias, norm, kv, qpad, gpad, delta, before, r0, r1, *refs):
    outs, (sums, result, query) = refs[:YS], refs[YS:]
    y, _, _, _ = place()

    @pl.when(y < SEQS)
    def _():
        sums[...] = before[...]
        backward_blocks(KEYS[2], turned, bias, norm, kv, qpad, gpad, delta, sums, result)
        query[...] = (sums[...] * HEAD_DIM ** (-0.5)).astype(bf16)
        for s, out in enumerate(outs):
            chunk = (y + s) % YS
            out[:HEAD_DIM] = query[:, aligned(chunk, PAIR)]
            for part, blocks in zip((r0, r1, result), KEYS):
                for block in blocks:
                    lane = (block - blocks[0]) * WIDE
                    slot = block % 2 * WIDE

                    @pl.when(chunk == block // 2)
                    def _():
                        out[HEAD_DIM:, slot : slot + WIDE] = part[:, lane : lane + WIDE]


def collect_kernel(*refs):
    pieces, keep, send = refs[:YS], refs[YS], refs[YS + 1]
    y, core, _, _ = place()
    for s, piece in enumerate(pieces):
        source = (y + YS - s) % YS

        @pl.when(source < SEQS)
        def _():
            lanes = aligned(seq_of(source), SPAN)
            keep[:, lanes] = piece[:, aligned(core, SPAN)]
            send[:, lanes] = piece[:, aligned(1 - core, SPAN)]


def finish_kernel(keep, got, q, k, v, whole):
    _, core, _, _ = place()
    for part, out in enumerate((q, k, v)):
        rows = slice(part * HEAD_DIM, (part + 1) * HEAD_DIM)
        whole[part, aligned(core, HEAD_DIM), :] = keep[rows, :]
        whole[part, aligned(1 - core, HEAD_DIM), :] = got[rows, :]
        out[...] = whole[part].T


def weight_grad_kernel(mine, theirs, o0, o1, o2, o3, *refs):
    outs, allg, allo, product = refs[:YS], refs[YS], refs[YS + 1], refs[YS + 2]
    y, core, _, x = place()
    for s, piece in enumerate((o0, o1, o2, o3)):
        allo[aligned((x + XS - s) % XS, HEAD_DIM), :] = piece[...]
    allg[:, aligned(core, TOKENS)] = mine[...]
    allg[:, aligned(1 - core, TOKENS)] = theirs[...]
    product[...] = dot(allg[...], allo[...], NT)
    for s, out in enumerate(outs):
        out[...] = product[aligned((y + s) % YS, CORES * WIDTH), :].astype(out.dtype)


def total_kernel(*refs):
    parts, (keep, send, whole) = refs[:YS], refs[YS:]
    _, core, _, _ = place()
    total = parts[0][...]
    for part in parts[1:]:
        total = total + part[...].astype(f32)
    whole[...] = total
    square = jnp.sum(jnp.sum(total * total, axis=0, keepdims=True), axis=1, keepdims=True)
    for half, out in ((core, keep), (1 - core, send)):
        out[:WIDTH] = whole[aligned(half, WIDTH), :]
        out[WIDTH:] = jnp.broadcast_to(square, (8, XS * HEAD_DIM))


def square_kernel(keep, got, *refs):
    outs, whole = refs[:XS], refs[XS]
    _, core, _, x = place()
    first = core == 0
    for block in range(XS):
        cols = slice(block * HEAD_DIM, (block + 1) * HEAD_DIM)
        a, b = keep[:WIDTH, cols], got[:WIDTH, cols]
        low, high = jnp.where(first, a, b), jnp.where(first, b, a)
        whole[:, block * WIDTH : (block + 1) * WIDTH] = jnp.concatenate([low, high], axis=1)
    values = whole[...]
    row_sum = lax.dot_general(
        jnp.ones((8, XS * WIDTH), f32),
        values * values,
        NT,
        precision=lax.Precision.HIGHEST,
        preferred_element_type=f32,
    )
    square = keep[WIDTH:, :WIDTH] + got[WIDTH:, :WIDTH]
    for s, out in enumerate(outs):
        out[:WIDTH] = whole[:, aligned((x + s) % XS, WIDTH)]
        out[WIDTH : WIDTH + 8] = row_sum
        out[WIDTH + 8 :] = square


def place_kernel(*refs):
    parts, (moment, grad, rows, cols) = refs[:XS], refs[XS:]
    _, _, _, x = place()
    square = jnp.zeros((8, WIDTH), f32)
    col = jnp.zeros((1, WIDTH), f32)
    for s, part in enumerate(parts):
        source = (x + XS - s) % XS
        values = part[:WIDTH]
        grad[aligned(source, WIDTH), :] = values
        rows[:, aligned(source, WIDTH)] = part[WIDTH : WIDTH + 8]
        square = square + part[WIDTH + 8 :]
        col = col + jnp.sum(values * values, axis=0, keepdims=True)
    rows[:, XS * WIDTH :] = square
    cols[:, :WIDTH] = jnp.broadcast_to(col, (8, WIDTH))
    held = jnp.sum(moment[...], axis=1, keepdims=True)
    cols[:, WIDTH:] = jnp.broadcast_to(held, (8, WIDTH))


def reduce_kernel(r0, r1, c0, c1, rows, cols):
    row = r0[...] + r1[...]
    rows[...] = row[:, : XS * WIDTH]
    cols[:, : 2 * WIDTH] = c0[...] + c1[...]
    cols[:, 2 * WIDTH :] = row[:, XS * WIDTH :]


def update_kernel(c0, c1, c2, c3, rows, grad, row_moment, col_moment, out, new_row, new_col):
    keep = 1.0 - moment_decay
    col = c0[...] + c1[...] + c2[...] + c3[...]
    row_square = rows[:1] / HD + square_floor
    col_square = col[:1, :WIDTH] / D + square_floor
    new_row[...] = moment_decay * row_moment[...] + keep * row_square
    new_col[...] = moment_decay * col_moment[...] + keep * col_square
    held, total = col[:1, WIDTH : 2 * WIDTH], col[:1, 2 * WIDTH :]
    mean = (moment_decay * held + keep * (total / HD + D * square_floor)) / D
    row = jnp.broadcast_to(new_row[...], (8, new_row.shape[1])).T[:, :1]
    out[...] = grad[...] * lax.rsqrt(row * new_col[...] / mean)


def together(arrays):
    return list(lax.optimization_barrier(tuple(arrays)))


def after(arrays, first):
    return together([*arrays, first])[:-1]


def body(queries, keys, values, grad_out, out_weight, tile_plan, row_moment, col_moment):
    flat = lambda a: a.reshape(TOKENS, WIDTH)
    ys = range(1, YS)
    xs = range(1, XS)

    turned, *pieces, keep, send = call(
        pack_kernel,
        [((WIDTH, TOKENS), bf16)]
        + [((WIDTH, WIDTH), bf16)] * XS
        + [((QKV + SEQS * TILES, TOKENS), bf16)] * 2,
        (flat(grad_out), out_weight, flat(queries), flat(keys), flat(values), tile_plan.T),
        scratch=[
            pltpu.VMEM((3 * WIDTH, TOKENS), bf16),
            pltpu.SemaphoreType.DMA((6,)),
            pltpu.VMEM((TOKENS, WIDTH), bf16),
            pltpu.VMEM((XS * WIDTH, WIDTH), bf16),
        ]
        + [pltpu.VMEM((TOKENS, WIDTH), bf16)] * 3
        + [pltpu.VMEM(tile_plan.shape[::-1], jnp.int32)],
        hbm=6,
        limit=62,
    )

    got = swap_core(send)
    packed = call(merge_kernel, [((QKV + TILES, PAIR), bf16)] * YS, (keep, got))
    turned, *packed = together([turned, *packed])
    packed = [packed[0]] + [send_y(packed[s], s) for s in ys]
    up, down = [turned, send_z(turned, 1)], [turned, send_z(turned, -1)]
    up.append(send_z(up[1], 1))
    down.append(send_z(down[1], -1))
    up.append(send_z(up[2], 1))
    down.append(send_z(down[2], -1))
    features = up + [send_z(up[3], 1)] + down[:0:-1]

    pieces = after(pieces, packed[1])
    packed = together([*packed, up[1], down[1]])[:YS]
    pieces = [pieces[0]] + [send_x(pieces[s], s) for s in xs]

    held = call(
        forward_kernel,
        [
            ((QKV, LEN), bf16),
            ((TILES, LEN), f32),
            ((8, LEN), f32),
            ((HEAD_DIM, LEN), bf16),
            ((LEN, 2 * HEAD_DIM), bf16),
        ]
        + [((HEAD_DIM, PAIR), bf16)] * YS,
        (*packed,),
        scratch=[
            pltpu.VMEM((2 * HEAD_DIM, LEN), bf16),
            pltpu.VMEM((TILES, BLOCK), f32),
            pltpu.VMEM((LEN, WIDE), f32),
        ],
        us=6.0,
    )
    held, outputs = held[:5], held[5:]

    outputs = call(
        join_kernel, [((HEAD_DIM + WIDTH, PAIR), bf16)] * YS, (*outputs, *pieces)
    )
    outputs = together([*outputs, up[2], down[2]])[:YS]
    outputs = [outputs[0]] + [send_y(outputs[s], s) for s in ys]
    outputs = together([*outputs, up[3], down[3]])[:YS]
    attn_out, weight = call(
        gather_kernel,
        [((HEAD_DIM, CORES * TOKENS), bf16), ((XS * WIDTH, YS * WIDTH), bf16)],
        (*outputs,),
    )
    attn_outs = [attn_out] + [send_x(attn_out, s) for s in xs]
    weights = [weight, swap_core(weight)]
    weights = together([*weights, *attn_outs[1:3]])[:2]

    allg, *partial = call(
        project_kernel,
        [((ZS * WIDTH, TOKENS), bf16), ((WIDTH, TOKENS), f32)] + [((WIDTH, TOKENS), bf16)] * 3,
        (*weights, *features),
        scratch=[pltpu.VMEM((XS * WIDTH, ROWS * WIDTH), bf16)],
    )
    theirs = swap_core(allg)
    partial = [partial[0]] + [send_x(partial[s], s) for s in xs]
    keep, send = call(
        cotangent_kernel,
        [((HEAD_DIM, TOKENS), bf16)] * 2,
        (*partial,),
        scratch=[pltpu.VMEM((WIDTH, TOKENS), bf16)],
    )
    grads = call(spread_kernel, [((HEAD_DIM, PAIR), bf16)] * YS, (keep, swap_core(send)))
    grads = [grads[0]] + [send_y(grads[s], s) for s in ys]

    block = (CORES * WIDTH, XS * HEAD_DIM)
    products = call(
        weight_grad_kernel,
        [(block, f32)] + [(block, bf16)] * (YS - 1),
        (allg, theirs, *attn_outs),
        scratch=[
            pltpu.VMEM((ZS * WIDTH, CORES * TOKENS), bf16),
            pltpu.VMEM((XS * HEAD_DIM, CORES * TOKENS), bf16),
            pltpu.VMEM((ZS * WIDTH, XS * HEAD_DIM), f32),
        ],
        limit=24,
    )
    products = together([*products, *partial[1:3]])[: len(products)]
    products = [products[0]] + [send_y(products[s], s) for s in ys]
    keep, send = call(
        total_kernel,
        [((WIDTH + 8, XS * HEAD_DIM), f32)] * 2,
        (*products,),
        scratch=[pltpu.VMEM(block, f32)],
    )
    squares = call(
        square_kernel,
        [((WIDTH + 16, WIDTH), f32)] * XS,
        (keep, swap_core(send)),
        scratch=[pltpu.VMEM((WIDTH, XS * WIDTH), f32)],
    )
    squares = [squares[0]] + [send_x(squares[s], s) for s in xs]
    turned, bias, norm, whole, kv = held
    sizes = [len(blocks) * WIDE for blocks in KEYS]
    qpad, gpad, delta, sums, first = call(
        first_backward_kernel,
        [
            ((2 * HEAD_DIM, LEN), bf16),
            ((2 * HEAD_DIM, LEN), bf16),
            ((8, LEN), f32),
            ((HEAD_DIM, LEN), f32),
            ((2 * HEAD_DIM, sizes[0]), bf16),
        ],
        (*grads, *held),
        us=4.0,
    )
    shared = (turned, bias, norm, kv, qpad, gpad, delta)
    squares = after(squares, sums)
    row_held = row_moment.reshape(1, -1)
    weight_grad, row_part, col_part = call(
        place_kernel,
        [((XS * WIDTH, WIDTH), f32), ((8, (XS + 1) * WIDTH), f32), ((8, 2 * WIDTH), f32)],
        (*squares, row_held),
    )


    col_other = swap_core(col_part)
    row_other = swap_z(row_part, 1)
    sums, *_ = together([sums, row_part, col_other])
    sums, second = call(
        second_backward_kernel,
        [((HEAD_DIM, LEN), f32), ((2 * HEAD_DIM, sizes[1]), bf16)],
        (*shared, sums),
        us=4.0,
    )
    row_part = row_part + row_other
    row_other = swap_z(row_part, 2)
    sums = after([sums], row_part)[0]
    results = call(
        last_backward_kernel,
        [((QKV, PAIR), bf16)] * YS,
        (*shared, sums, first, second),
        scratch=[
            pltpu.VMEM((HEAD_DIM, LEN), f32),
            pltpu.VMEM((2 * HEAD_DIM, sizes[2]), bf16),
            pltpu.VMEM((HEAD_DIM, LEN), bf16),
        ],
        us=4.0,
    )
    row_part = row_part + row_other
    results = after(results, row_part)
    row_other = swap_z(row_part, 4)
    row_sum, col_part = call(
        reduce_kernel,
        [((8, XS * WIDTH), f32), ((8, 3 * WIDTH), f32)],
        (row_part, row_other, col_part, col_other),
    )
    col_parts = [col_part] + [send_y(col_part, s) for s in ys]
    results = [results[0]] + [send_y(results[s], s) for s in ys]
    results = together([*results, *col_parts[1:]])[:YS]
    keep, send = call(collect_kernel, [((QKV, TOKENS), bf16)] * 2, (*results,))
    query_grad, key_grad, value_grad = call(
        finish_kernel,
        [((TOKENS, WIDTH), bf16)] * 3,
        (keep, swap_core(send)),
        scratch=[pltpu.VMEM((3, WIDTH, TOKENS), bf16)],
    )

    update, new_row, new_col = call(
        update_kernel,
        [((XS * WIDTH, WIDTH), f32), ((1, XS * WIDTH), f32), ((1, WIDTH), f32)],
        (*col_parts, row_sum, weight_grad, row_held, col_moment.reshape(1, -1)),
    )
    return (
        query_grad.reshape(queries.shape),
        key_grad.reshape(keys.shape),
        value_grad.reshape(values.shape),
        update,
        new_row.reshape(-1),
        new_col.reshape(-1),
    )


def solution(mesh):
    in_specs = (
        P(None, "row", "col"),
        P(None, "row", "col"),
        P(None, "row", "col"),
        P(None, "row", "col"),
        P("row", "col"),
        P("row", None),
        P("row"),
        P("col"),
    )
    out_specs = (
        P(None, "row", "col"),
        P(None, "row", "col"),
        P(None, "row", "col"),
        P("row", "col"),
        P("row"),
        P("col"),
    )
    return jax.shard_map(body, mesh=mesh, in_specs=in_specs, out_specs=out_specs, check_vma=False)
```

```python
import jax
import jax.numpy as jnp
from jax import lax
from jax.experimental import pallas as pl
from jax.experimental.pallas import tpu as pltpu
from jax.sharding import PartitionSpec as P

D = 4096
HEAD_DIM = 64
HD = 4096
LEN = 2048
BLOCK = 128
SEQS = 3
ROWS = 8
YS = 4
CORES = 2
ZS = 8
XS = 4
SPAN = LEN // ROWS
WIDTH = 128
TOKENS = SEQS * SPAN
PAIR = CORES * SPAN
QKV = 3 * HEAD_DIM
TILES = LEN // BLOCK
WIDE = 256
KEYS = (range(0, 2), range(2, 4), range(4, 8))

masked_score = -1e30
moment_decay = 0.9
square_floor = 1e-30

bf16 = jnp.bfloat16
f32 = jnp.float32
NN = (((1,), (0,)), ((), ()))
NT = (((1,), (1,)), ((), ()))


def dot(a, b, dims=NN):
    return lax.dot_general(a, b, dims, preferred_element_type=f32)


def y_pairs(shift):
    return [(y * CORES + c, (y + shift) % YS * CORES + c) for y in range(YS) for c in range(CORES)]


def z_pairs(shift):
    return [(z * XS + x, (z + shift) % ZS * XS + x) for z in range(ZS) for x in range(XS)]


def x_pairs(shift):
    return [(z * XS + x, z * XS + (x + shift) % XS) for z in range(ZS) for x in range(XS)]


def send_y(a, shift):
    return lax.ppermute(a, "row", y_pairs(shift))


def send_z(a, shift):
    return lax.ppermute(a, "col", z_pairs(shift))


def send_x(a, shift):
    return lax.ppermute(a, "col", x_pairs(shift))


def swap_core(a):
    return lax.ppermute(a, "row", [(j, j ^ 1) for j in range(ROWS)])


def swap_z(a, bit):
    pairs = [(z * XS + x, (z ^ bit) * XS + x) for z in range(ZS) for x in range(XS)]
    return lax.ppermute(a, "col", pairs)


def aligned(index, size):
    return pl.ds(pl.multiple_of(index * size, size), size)


def call(kernel, outs, args, scratch=(), hbm=0, us=0.5, limit=16):
    spaces = [pltpu.HBM] * hbm
    space = lambda i: spaces[i] if i < len(spaces) else pltpu.VMEM
    return pl.pallas_call(
        kernel,
        out_shape=[jax.ShapeDtypeStruct(s, t) for s, t in outs],
        in_specs=[pl.BlockSpec(memory_space=space(i)) for i in range(len(args))],
        out_specs=[pl.BlockSpec(memory_space=pltpu.VMEM) for _ in outs],
        scratch_shapes=list(scratch),
        compiler_params=pltpu.CompilerParams(vmem_limit_bytes=limit * 2**20),
        cost_estimate=pl.CostEstimate(
            flops=int(us * 1.1e9), bytes_accessed=int(us * 3e6), transcendentals=0
        ),
    )(*args,)


def place():
    row, col = lax.axis_index("row"), lax.axis_index("col")
    return row // CORES, row % CORES, col // XS, col % XS


def seq_of(y):
    return jnp.minimum(y, SEQS - 1)


def pack_kernel(*refs):
    sources, (gt, w0, w1, w2, w3, keep, send) = refs[:6], refs[6:13]
    turned, sem, held = refs[13], refs[14], refs[15:]
    _, core, _, x = place()
    copies = [pltpu.make_async_copy(a, b, sem.at[i]) for i, (a, b) in enumerate(zip(sources, held))]
    for copy in copies:
        copy.start()
    for copy in copies:
        copy.wait()
    g, w, q, k, v, plan = held
    gt[...] = g[...].T
    for s, out in enumerate((w0, w1, w2, w3)):
        out[...] = w[aligned((x + s) % XS, WIDTH), :].T
    turned[:WIDTH] = (q[...].astype(f32) * HEAD_DIM ** (-0.5)).astype(bf16).T
    turned[WIDTH : 2 * WIDTH] = k[...].T
    turned[2 * WIDTH :] = v[...].T
    count = plan.shape[1]
    rows = lax.broadcasted_iota(jnp.int32, (SEQS * TILES, count), 0)
    lanes = lax.broadcasted_iota(jnp.int32, (WIDTH, count), 0)
    here = (plan[0:1, :] * TILES + plan[2:3, :] == rows).astype(f32)
    there = (plan[1:2, :] == lanes).astype(f32)
    member = dot(here.astype(bf16), there.astype(bf16), NT)
    for head, out in ((core, keep), (1 - core, send)):
        for part in range(3):
            rows = pl.ds(pl.multiple_of(part * WIDTH + head * HEAD_DIM, HEAD_DIM), HEAD_DIM)
            out[part * HEAD_DIM : (part + 1) * HEAD_DIM] = turned[rows, :]
        out[QKV:, :WIDTH] = member.astype(bf16)


def merge_kernel(keep, got, *outs):
    y, core, _, _ = place()
    for s, out in enumerate(outs):
        seq = seq_of((y + s) % YS)
        out[:QKV, aligned(core, SPAN)] = keep[:QKV, aligned(seq, SPAN)]
        out[:QKV, aligned(1 - core, SPAN)] = got[:QKV, aligned(seq, SPAN)]
        rows = pl.ds(pl.multiple_of(QKV + seq * TILES, TILES), TILES)
        out[QKV:, :WIDTH] = keep[rows, :WIDTH] + got[rows, :WIDTH]


def causal_bias():
    key = lax.broadcasted_iota(jnp.int32, (WIDE, WIDE), 0)
    query = lax.broadcasted_iota(jnp.int32, (WIDE, WIDE), 1)
    return jnp.where(key <= query, 0.0, masked_score).astype(f32)


def biased(score, bias, kb, qb):
    lanes = slice(qb * WIDE, (qb + 1) * WIDE)
    per = WIDE // BLOCK
    parts = []
    for t in range(per):
        row = bias[kb * per + t : kb * per + t + 1, lanes]
        parts.append(score[t * BLOCK : (t + 1) * BLOCK] + row)
    score = jnp.concatenate(parts, axis=0)
    if kb == qb:
        score = score + causal_bias()
    return score


def span_of(b):
    return slice(b * WIDE, (b + 1) * WIDE)


def forward_kernel(*refs):
    pieces, refs = refs[:YS], refs[YS:]
    turned, bias, norm, whole, kv, outs = *refs[:5], refs[5 : 5 + YS]
    qpad, member, scores = refs[5 + YS :]
    y, _, _, _ = place()

    @pl.when(y < SEQS)
    def _():
        member[...] = jnp.zeros_like(member)
        for s, piece in enumerate(pieces):
            turned[:, aligned((y + YS - s) % YS, PAIR)] = piece[:QKV]
            member[...] += piece[QKV:, :BLOCK].astype(f32)
        tile = lax.broadcasted_iota(jnp.int32, (BLOCK, LEN), 0)
        lane = lax.broadcasted_iota(jnp.int32, (BLOCK, LEN), 1) // BLOCK
        spread = jnp.where(tile == lane, 1.0, 0.0).astype(bf16)
        here = dot(member[...].astype(bf16), spread)
        bias[...] = jnp.where(here > 0.5, 0.0, masked_score)
        qpad[:HEAD_DIM] = turned[:HEAD_DIM]
        qpad[HEAD_DIM:] = jnp.zeros((HEAD_DIM, LEN), bf16)
        for b in range(LEN // WIDE):
            kv[span_of(b)] = turned[HEAD_DIM:, span_of(b)].T
        for qb in range(LEN // WIDE):
            qs = span_of(qb)
            query = qpad[:, qs]
            top = jnp.full((1, WIDE), 2 * masked_score, f32)
            for kb in range(qb + 1):
                score = biased(dot(kv[span_of(kb)], query), bias, kb, qb)
                scores[span_of(kb)] = score
                top = jnp.maximum(top, jnp.max(score, axis=0, keepdims=True))
            total = jnp.zeros((1, WIDE), f32)
            acc = jnp.zeros((HEAD_DIM, WIDE), f32)
            for kb in range(qb + 1):
                probs = jnp.exp(scores[span_of(kb)] - top)
                total += jnp.sum(probs, axis=0, keepdims=True)
                acc += dot(turned[2 * HEAD_DIM :, span_of(kb)], probs.astype(bf16))
            whole[:, qs] = (acc / total).astype(bf16)
            norm[:, qs] = jnp.broadcast_to(top + jnp.log(total), (8, WIDE))
        for s, out in enumerate(outs):
            out[...] = whole[:, aligned((y + s) % YS, PAIR)]


def join_kernel(*refs):
    pieces, blocks, outs = refs[:YS], refs[YS : YS + XS], refs[YS + XS :]
    _, _, _, x = place()
    for piece, out in zip(pieces, outs):
        out[:HEAD_DIM] = piece[...]
        for s, block in enumerate(blocks):
            out[HEAD_DIM:, aligned((x + XS - s) % XS, WIDTH)] = block[...]


def gather_kernel(*refs):
    pieces, out, weight = refs[:YS], refs[YS], refs[YS + 1]
    y, _, _, _ = place()
    for s, piece in enumerate(pieces):
        source = (y + YS - s) % YS
        for block in range(XS):
            cols = slice(block * WIDTH, (block + 1) * WIDTH)
            weight[cols, aligned(source, WIDTH)] = piece[HEAD_DIM:, cols]

        @pl.when(source < SEQS)
        def _():
            seq = seq_of(source)
            for core in range(CORES):
                lanes = pl.ds(pl.multiple_of(core * TOKENS + seq * SPAN, SPAN), SPAN)
                out[:, lanes] = piece[:HEAD_DIM, core * SPAN : (core + 1) * SPAN]


def project_kernel(mine, theirs, *refs):
    gs, (allg, own, p1, p2, p3, allw) = refs[:ZS], refs[ZS:]
    _, core, z, x = place()
    for k in range(YS):
        cols = slice(k * WIDTH, (k + 1) * WIDTH)
        allw[:, aligned(k * CORES + core, WIDTH)] = mine[:, cols]
        allw[:, aligned(k * CORES + 1 - core, WIDTH)] = theirs[:, cols]
    for k in range(ZS):
        allg[aligned((z + ZS - k) % ZS, WIDTH), :] = gs[k][...]
    own[...] = dot(allw[aligned(x, WIDTH), :], allg[...])
    for s, out in enumerate((p1, p2, p3)):
        out[...] = dot(allw[aligned((x + s + 1) % XS, WIDTH), :], allg[...]).astype(bf16)


def cotangent_kernel(own, p1, p2, p3, keep, send, whole):
    _, core, _, _ = place()
    total = own[...] + p1[...].astype(f32) + p2[...].astype(f32) + p3[...].astype(f32)
    whole[...] = total.astype(bf16)
    keep[...] = whole[aligned(core, HEAD_DIM), :]
    send[...] = whole[aligned(1 - core, HEAD_DIM), :]


def spread_kernel(keep, got, *outs):
    y, core, _, _ = place()
    for s, out in enumerate(outs):
        seq = seq_of((y + s) % YS)
        out[:, aligned(core, SPAN)] = keep[:, aligned(seq, SPAN)]
        out[:, aligned(1 - core, SPAN)] = got[:, aligned(seq, SPAN)]


def backward_blocks(blocks, turned, bias, norm, kv, qpad, gpad, delta, sums, result):
    for kb in blocks:
        ks = span_of(kb)
        here = slice((kb - blocks[0]) * WIDE, (kb - blocks[0] + 1) * WIDE)
        key_value = kv[ks]
        key_t = turned[HEAD_DIM : 2 * HEAD_DIM, ks]
        key_acc = jnp.zeros((HEAD_DIM, WIDE), f32)
        value_acc = jnp.zeros((HEAD_DIM, WIDE), f32)
        for qb in range(kb, LEN // WIDE):
            qs = span_of(qb)
            score = biased(dot(key_value, qpad[:, qs]), bias, kb, qb)
            probs = jnp.exp(score - norm[:1, qs])
            dprobs = dot(key_value, gpad[:, qs])
            dscore = (probs * (dprobs - delta[:1, qs])).astype(bf16)
            value_acc += dot(gpad[HEAD_DIM:, qs], probs.astype(bf16), NT)
            key_acc += dot(turned[:HEAD_DIM, qs], dscore, NT)
            part = dot(key_t, dscore)
            if kb == 0:
                sums[:, qs] = part
            else:
                sums[:, qs] += part
        result[:HEAD_DIM, here] = key_acc.astype(bf16)
        result[HEAD_DIM:, here] = value_acc.astype(bf16)


def first_backward_kernel(*refs):
    pieces, (turned, bias, norm, whole, kv) = refs[:YS], refs[YS : YS + 5]
    qpad, gpad, delta, sums, result = refs[YS + 5 :]
    y, _, _, _ = place()

    @pl.when(y < SEQS)
    def _():
        qpad[:HEAD_DIM] = turned[:HEAD_DIM]
        qpad[HEAD_DIM:] = jnp.zeros((HEAD_DIM, LEN), bf16)
        gpad[:HEAD_DIM] = jnp.zeros((HEAD_DIM, LEN), bf16)
        for s, piece in enumerate(pieces):
            gpad[HEAD_DIM:, aligned((y + YS - s) % YS, PAIR)] = piece[...]
        products = gpad[HEAD_DIM:].astype(f32) * whole[...].astype(f32)
        delta[...] = jnp.broadcast_to(jnp.sum(products, axis=0, keepdims=True), (8, LEN))
        backward_blocks(KEYS[0], turned, bias, norm, kv, qpad, gpad, delta, sums, result)


def second_backward_kernel(turned, bias, norm, kv, qpad, gpad, delta, before, sums, result):
    y, _, _, _ = place()

    @pl.when(y < SEQS)
    def _():
        sums[...] = before[...]
        backward_blocks(KEYS[1], turned, bias, norm, kv, qpad, gpad, delta, sums, result)


def last_backward_kernel(turned, bias, norm, kv, qpad, gpad, delta, before, r0, r1, *refs):
    outs, (sums, result, query) = refs[:YS], refs[YS:]
    y, _, _, _ = place()

    @pl.when(y < SEQS)
    def _():
        sums[...] = before[...]
        backward_blocks(KEYS[2], turned, bias, norm, kv, qpad, gpad, delta, sums, result)
        query[...] = (sums[...] * HEAD_DIM ** (-0.5)).astype(bf16)
        for s, out in enumerate(outs):
            chunk = (y + s) % YS
            out[:HEAD_DIM] = query[:, aligned(chunk, PAIR)]
            for part, blocks in zip((r0, r1, result), KEYS):
                for block in blocks:
                    lane = (block - blocks[0]) * WIDE
                    slot = block % 2 * WIDE

                    @pl.when(chunk == block // 2)
                    def _():
                        out[HEAD_DIM:, slot : slot + WIDE] = part[:, lane : lane + WIDE]


def collect_kernel(*refs):
    pieces, keep, send = refs[:YS], refs[YS], refs[YS + 1]
    y, core, _, _ = place()
    for s, piece in enumerate(pieces):
        source = (y + YS - s) % YS

        @pl.when(source < SEQS)
        def _():
            lanes = aligned(seq_of(source), SPAN)
            keep[:, lanes] = piece[:, aligned(core, SPAN)]
            send[:, lanes] = piece[:, aligned(1 - core, SPAN)]


def finish_kernel(keep, got, q, k, v, whole):
    _, core, _, _ = place()
    for part, out in enumerate((q, k, v)):
        rows = slice(part * HEAD_DIM, (part + 1) * HEAD_DIM)
        whole[part, aligned(core, HEAD_DIM), :] = keep[rows, :]
        whole[part, aligned(1 - core, HEAD_DIM), :] = got[rows, :]
        out[...] = whole[part].T


def weight_grad_kernel(mine, theirs, o0, o1, o2, o3, *refs):
    outs, allg, allo, product = refs[:YS], refs[YS], refs[YS + 1], refs[YS + 2]
    y, core, _, x = place()
    for s, piece in enumerate((o0, o1, o2, o3)):
        allo[aligned((x + XS - s) % XS, HEAD_DIM), :] = piece[...]
    allg[:, aligned(core, TOKENS)] = mine[...]
    allg[:, aligned(1 - core, TOKENS)] = theirs[...]
    product[...] = dot(allg[...], allo[...], NT)
    for s, out in enumerate(outs):
        out[...] = product[aligned((y + s) % YS, CORES * WIDTH), :].astype(out.dtype)


def total_kernel(*refs):
    parts, (keep, send, whole) = refs[:YS], refs[YS:]
    _, core, _, _ = place()
    total = parts[0][...]
    for part in parts[1:]:
        total = total + part[...].astype(f32)
    whole[...] = total
    square = jnp.sum(jnp.sum(total * total, axis=0, keepdims=True), axis=1, keepdims=True)
    for half, out in ((core, keep), (1 - core, send)):
        out[:WIDTH] = whole[aligned(half, WIDTH), :]
        out[WIDTH:] = jnp.broadcast_to(square, (8, XS * HEAD_DIM))


def square_kernel(keep, got, *refs):
    outs, whole = refs[:XS], refs[XS]
    _, core, _, x = place()
    first = core == 0
    for block in range(XS):
        cols = slice(block * HEAD_DIM, (block + 1) * HEAD_DIM)
        a, b = keep[:WIDTH, cols], got[:WIDTH, cols]
        low, high = jnp.where(first, a, b), jnp.where(first, b, a)
        whole[:, block * WIDTH : (block + 1) * WIDTH] = jnp.concatenate([low, high], axis=1)
    values = whole[...]
    row_sum = lax.dot_general(
        jnp.ones((8, XS * WIDTH), f32),
        values * values,
        NT,
        precision=lax.Precision.HIGHEST,
        preferred_element_type=f32,
    )
    square = keep[WIDTH:, :WIDTH] + got[WIDTH:, :WIDTH]
    for s, out in enumerate(outs):
        out[:WIDTH] = whole[:, aligned((x + s) % XS, WIDTH)]
        out[WIDTH : WIDTH + 8] = row_sum
        out[WIDTH + 8 :] = square


def place_kernel(*refs):
    parts, (moment, grad, rows, cols) = refs[:XS], refs[XS:]
    _, _, _, x = place()
    square = jnp.zeros((8, WIDTH), f32)
    col = jnp.zeros((1, WIDTH), f32)
    for s, part in enumerate(parts):
        source = (x + XS - s) % XS
        values = part[:WIDTH]
        grad[aligned(source, WIDTH), :] = values
        rows[:, aligned(source, WIDTH)] = part[WIDTH : WIDTH + 8]
        square = square + part[WIDTH + 8 :]
        col = col + jnp.sum(values * values, axis=0, keepdims=True)
    rows[:, XS * WIDTH :] = square
    cols[:, :WIDTH] = jnp.broadcast_to(col, (8, WIDTH))
    held = jnp.sum(moment[...], axis=1, keepdims=True)
    cols[:, WIDTH:] = jnp.broadcast_to(held, (8, WIDTH))


def reduce_kernel(r0, r1, c0, c1, rows, cols):
    row = r0[...] + r1[...]
    rows[...] = row[:, : XS * WIDTH]
    cols[:, : 2 * WIDTH] = c0[...] + c1[...]
    cols[:, 2 * WIDTH :] = row[:, XS * WIDTH :]


def update_kernel(c0, c1, c2, c3, rows, grad, row_moment, col_moment, out, new_row, new_col):
    keep = 1.0 - moment_decay
    col = c0[...] + c1[...] + c2[...] + c3[...]
    row_square = rows[:1] / HD + square_floor
    col_square = col[:1, :WIDTH] / D + square_floor
    new_row[...] = moment_decay * row_moment[...] + keep * row_square
    new_col[...] = moment_decay * col_moment[...] + keep * col_square
    held, total = col[:1, WIDTH : 2 * WIDTH], col[:1, 2 * WIDTH :]
    mean = (moment_decay * held + keep * (total / HD + D * square_floor)) / D
    row = jnp.broadcast_to(new_row[...], (8, new_row.shape[1])).T[:, :1]
    out[...] = grad[...] * lax.rsqrt(row * new_col[...] / mean)


def together(arrays):
    return list(lax.optimization_barrier(tuple(arrays)))


def after(arrays, first):
    return together([*arrays, first])[:-1]


def body(queries, keys, values, grad_out, out_weight, tile_plan, row_moment, col_moment):
    flat = lambda a: a.reshape(TOKENS, WIDTH)
    ys = range(1, YS)
    xs = range(1, XS)

    turned, *pieces, keep, send = call(
        pack_kernel,
        [((WIDTH, TOKENS), bf16)]
        + [((WIDTH, WIDTH), bf16)] * XS
        + [((QKV + SEQS * TILES, TOKENS), bf16)] * 2,
        (flat(grad_out), out_weight, flat(queries), flat(keys), flat(values), tile_plan.T),
        scratch=[
            pltpu.VMEM((3 * WIDTH, TOKENS), bf16),
            pltpu.SemaphoreType.DMA((6,)),
            pltpu.VMEM((TOKENS, WIDTH), bf16),
            pltpu.VMEM((XS * WIDTH, WIDTH), bf16),
        ]
        + [pltpu.VMEM((TOKENS, WIDTH), bf16)] * 3
        + [pltpu.VMEM(tile_plan.shape[::-1], jnp.int32)],
        hbm=6,
        limit=61,
    )

    got = swap_core(send)
    packed = call(merge_kernel, [((QKV + TILES, PAIR), bf16)] * YS, (keep, got))
    turned, *packed = together([turned, *packed])
    packed = [packed[0]] + [send_y(packed[s], s) for s in ys]
    up, down = [turned, send_z(turned, 1)], [turned, send_z(turned, -1)]
    up.append(send_z(up[1], 1))
    down.append(send_z(down[1], -1))
    up.append(send_z(up[2], 1))
    down.append(send_z(down[2], -1))
    features = up + [send_z(up[3], 1)] + down[:0:-1]

    pieces = after(pieces, packed[1])
    packed = together([*packed, up[1], down[1]])[:YS]
    pieces = [pieces[0]] + [send_x(pieces[s], s) for s in xs]

    held = call(
        forward_kernel,
        [
            ((QKV, LEN), bf16),
            ((TILES, LEN), f32),
            ((8, LEN), f32),
            ((HEAD_DIM, LEN), bf16),
            ((LEN, 2 * HEAD_DIM), bf16),
        ]
        + [((HEAD_DIM, PAIR), bf16)] * YS,
        (*packed,),
        scratch=[
            pltpu.VMEM((2 * HEAD_DIM, LEN), bf16),
            pltpu.VMEM((TILES, BLOCK), f32),
            pltpu.VMEM((LEN, WIDE), f32),
        ],
        us=6.0,
    )
    held, outputs = held[:5], held[5:]

    outputs = call(
        join_kernel, [((HEAD_DIM + WIDTH, PAIR), bf16)] * YS, (*outputs, *pieces)
    )
    outputs = together([*outputs, up[2], down[2]])[:YS]
    outputs = [outputs[0]] + [send_y(outputs[s], s) for s in ys]
    outputs = together([*outputs, up[3], down[3]])[:YS]
    attn_out, weight = call(
        gather_kernel,
        [((HEAD_DIM, CORES * TOKENS), bf16), ((XS * WIDTH, YS * WIDTH), bf16)],
        (*outputs,),
    )
    attn_outs = [attn_out] + [send_x(attn_out, s) for s in xs]
    weights = [weight, swap_core(weight)]
    weights = together([*weights, *attn_outs[1:]])[:2]

    allg, *partial = call(
        project_kernel,
        [((ZS * WIDTH, TOKENS), bf16), ((WIDTH, TOKENS), f32)] + [((WIDTH, TOKENS), bf16)] * 3,
        (*weights, *features),
        scratch=[pltpu.VMEM((XS * WIDTH, ROWS * WIDTH), bf16)],
    )
    theirs = swap_core(allg)
    partial = [partial[0]] + [send_x(partial[s], s) for s in xs]
    keep, send = call(
        cotangent_kernel,
        [((HEAD_DIM, TOKENS), bf16)] * 2,
        (*partial,),
        scratch=[pltpu.VMEM((WIDTH, TOKENS), bf16)],
    )
    grads = call(spread_kernel, [((HEAD_DIM, PAIR), bf16)] * YS, (keep, swap_core(send)))
    grads = [grads[0]] + [send_y(grads[s], s) for s in ys]

    block = (CORES * WIDTH, XS * HEAD_DIM)
    products = call(
        weight_grad_kernel,
        [(block, f32)] + [(block, bf16)] * (YS - 1),
        (allg, theirs, *attn_outs),
        scratch=[
            pltpu.VMEM((ZS * WIDTH, CORES * TOKENS), bf16),
            pltpu.VMEM((XS * HEAD_DIM, CORES * TOKENS), bf16),
            pltpu.VMEM((ZS * WIDTH, XS * HEAD_DIM), f32),
        ],
        limit=24,
        us=12.0,
    )
    products = [products[0]] + [send_y(products[s], s) for s in ys]
    keep, send = call(
        total_kernel,
        [((WIDTH + 8, XS * HEAD_DIM), f32)] * 2,
        (*products,),
        scratch=[pltpu.VMEM(block, f32)],
    )
    squares = call(
        square_kernel,
        [((WIDTH + 16, WIDTH), f32)] * XS,
        (keep, swap_core(send)),
        scratch=[pltpu.VMEM((WIDTH, XS * WIDTH), f32)],
    )
    squares = [squares[0]] + [send_x(squares[s], s) for s in xs]
    turned, bias, norm, whole, kv = held
    sizes = [len(blocks) * WIDE for blocks in KEYS]
    qpad, gpad, delta, sums, first = call(
        first_backward_kernel,
        [
            ((2 * HEAD_DIM, LEN), bf16),
            ((2 * HEAD_DIM, LEN), bf16),
            ((8, LEN), f32),
            ((HEAD_DIM, LEN), f32),
            ((2 * HEAD_DIM, sizes[0]), bf16),
        ],
        (*grads, *held),
        us=4.0,
    )
    shared = (turned, bias, norm, kv, qpad, gpad, delta)
    squares = after(squares, sums)
    row_held = row_moment.reshape(1, -1)
    weight_grad, row_part, col_part = call(
        place_kernel,
        [((XS * WIDTH, WIDTH), f32), ((8, (XS + 1) * WIDTH), f32), ((8, 2 * WIDTH), f32)],
        (*squares, row_held),
    )


    col_other = swap_core(col_part)
    row_other = swap_z(row_part, 1)
    sums, *_ = together([sums, row_part, col_other])
    sums, second = call(
        second_backward_kernel,
        [((HEAD_DIM, LEN), f32), ((2 * HEAD_DIM, sizes[1]), bf16)],
        (*shared, sums),
        us=4.0,
    )
    row_part = row_part + row_other
    row_other = swap_z(row_part, 2)
    sums = after([sums], row_part)[0]
    results = call(
        last_backward_kernel,
        [((QKV, PAIR), bf16)] * YS,
        (*shared, sums, first, second),
        scratch=[
            pltpu.VMEM((HEAD_DIM, LEN), f32),
            pltpu.VMEM((2 * HEAD_DIM, sizes[2]), bf16),
            pltpu.VMEM((HEAD_DIM, LEN), bf16),
        ],
        us=4.0,
    )
    row_part = row_part + row_other
    results = after(results, row_part)
    row_other = swap_z(row_part, 4)
    row_sum, col_part = call(
        reduce_kernel,
        [((8, XS * WIDTH), f32), ((8, 3 * WIDTH), f32)],
        (row_part, row_other, col_part, col_other),
    )
    col_parts = [col_part] + [send_y(col_part, s) for s in ys]
    results = [results[0]] + [send_y(results[s], s) for s in ys]
    results = together([*results, *col_parts[1:]])[:YS]
    keep, send = call(collect_kernel, [((QKV, TOKENS), bf16)] * 2, (*results,))
    query_grad, key_grad, value_grad = call(
        finish_kernel,
        [((TOKENS, WIDTH), bf16)] * 3,
        (keep, swap_core(send)),
        scratch=[pltpu.VMEM((3, WIDTH, TOKENS), bf16)],
    )

    update, new_row, new_col = call(
        update_kernel,
        [((XS * WIDTH, WIDTH), f32), ((1, XS * WIDTH), f32), ((1, WIDTH), f32)],
        (*col_parts, row_sum, weight_grad, row_held, col_moment.reshape(1, -1)),
    )
    return (
        query_grad.reshape(queries.shape),
        key_grad.reshape(keys.shape),
        value_grad.reshape(values.shape),
        update,
        new_row.reshape(-1),
        new_col.reshape(-1),
    )


def solution(mesh):
    in_specs = (
        P(None, "row", "col"),
        P(None, "row", "col"),
        P(None, "row", "col"),
        P(None, "row", "col"),
        P("row", "col"),
        P("row", None),
        P("row"),
        P("col"),
    )
    out_specs = (
        P(None, "row", "col"),
        P(None, "row", "col"),
        P(None, "row", "col"),
        P("row", "col"),
        P("row"),
        P("col"),
    )
    return jax.shard_map(body, mesh=mesh, in_specs=in_specs, out_specs=out_specs, check_vma=False)
```

```python
import jax
import jax.numpy as jnp
from jax import lax
from jax.experimental import pallas as pl
from jax.experimental.pallas import tpu as pltpu
from jax.sharding import PartitionSpec as P

D = 4096
HEAD_DIM = 64
HD = 4096
LEN = 2048
BLOCK = 128
SEQS = 3
ROWS = 8
YS = 4
CORES = 2
ZS = 8
XS = 4
SPAN = LEN // ROWS
WIDTH = 128
TOKENS = SEQS * SPAN
PAIR = CORES * SPAN
QKV = 3 * HEAD_DIM
TILES = LEN // BLOCK
WIDE = 256
KEYS = (range(0, 2), range(2, 4), range(4, 8))

masked_score = -1e30
moment_decay = 0.9
square_floor = 1e-30

bf16 = jnp.bfloat16
f32 = jnp.float32
NN = (((1,), (0,)), ((), ()))
NT = (((1,), (1,)), ((), ()))


def dot(a, b, dims=NN):
    return lax.dot_general(a, b, dims, preferred_element_type=f32)


def y_pairs(shift):
    return [(y * CORES + c, (y + shift) % YS * CORES + c) for y in range(YS) for c in range(CORES)]


def z_pairs(shift):
    return [(z * XS + x, (z + shift) % ZS * XS + x) for z in range(ZS) for x in range(XS)]


def x_pairs(shift):
    return [(z * XS + x, z * XS + (x + shift) % XS) for z in range(ZS) for x in range(XS)]


def send_y(a, shift):
    return lax.ppermute(a, "row", y_pairs(shift))


def send_z(a, shift):
    return lax.ppermute(a, "col", z_pairs(shift))


def send_x(a, shift):
    return lax.ppermute(a, "col", x_pairs(shift))


def swap_core(a):
    return lax.ppermute(a, "row", [(j, j ^ 1) for j in range(ROWS)])


def swap_z(a, bit):
    pairs = [(z * XS + x, (z ^ bit) * XS + x) for z in range(ZS) for x in range(XS)]
    return lax.ppermute(a, "col", pairs)


def aligned(index, size):
    return pl.ds(pl.multiple_of(index * size, size), size)


def call(kernel, outs, args, scratch=(), hbm=0, us=0.5, limit=16):
    spaces = [pltpu.HBM] * hbm
    space = lambda i: spaces[i] if i < len(spaces) else pltpu.VMEM
    return pl.pallas_call(
        kernel,
        out_shape=[jax.ShapeDtypeStruct(s, t) for s, t in outs],
        in_specs=[pl.BlockSpec(memory_space=space(i)) for i in range(len(args))],
        out_specs=[pl.BlockSpec(memory_space=pltpu.VMEM) for _ in outs],
        scratch_shapes=list(scratch),
        compiler_params=pltpu.CompilerParams(vmem_limit_bytes=limit * 2**20),
        cost_estimate=pl.CostEstimate(
            flops=int(us * 1.1e9), bytes_accessed=int(us * 3e6), transcendentals=0
        ),
    )(*args,)


def place():
    row, col = lax.axis_index("row"), lax.axis_index("col")
    return row // CORES, row % CORES, col // XS, col % XS


def seq_of(y):
    return jnp.minimum(y, SEQS - 1)


def pack_kernel(*refs):
    sources, (gt, w0, w1, w2, w3, keep, send) = refs[:6], refs[6:13]
    turned, sem, held = refs[13], refs[14], refs[15:]
    _, core, _, x = place()
    copies = [pltpu.make_async_copy(a, b, sem.at[i]) for i, (a, b) in enumerate(zip(sources, held))]
    for copy in copies:
        copy.start()
    for copy in copies:
        copy.wait()
    g, w, q, k, v, plan = held
    gt[...] = g[...].T
    for s, out in enumerate((w0, w1, w2, w3)):
        out[...] = w[aligned((x + s) % XS, WIDTH), :].T
    turned[:WIDTH] = (q[...].astype(f32) * HEAD_DIM ** (-0.5)).astype(bf16).T
    turned[WIDTH : 2 * WIDTH] = k[...].T
    turned[2 * WIDTH :] = v[...].T
    count = plan.shape[1]
    rows = lax.broadcasted_iota(jnp.int32, (SEQS * TILES, count), 0)
    lanes = lax.broadcasted_iota(jnp.int32, (WIDTH, count), 0)
    here = (plan[0:1, :] * TILES + plan[2:3, :] == rows).astype(f32)
    there = (plan[1:2, :] == lanes).astype(f32)
    member = dot(here.astype(bf16), there.astype(bf16), NT)
    for head, out in ((core, keep), (1 - core, send)):
        for part in range(3):
            rows = pl.ds(pl.multiple_of(part * WIDTH + head * HEAD_DIM, HEAD_DIM), HEAD_DIM)
            out[part * HEAD_DIM : (part + 1) * HEAD_DIM] = turned[rows, :]
        out[QKV:, :WIDTH] = member.astype(bf16)


def merge_kernel(keep, got, *outs):
    y, core, _, _ = place()
    for s, out in enumerate(outs):
        seq = seq_of((y + s) % YS)
        out[:QKV, aligned(core, SPAN)] = keep[:QKV, aligned(seq, SPAN)]
        out[:QKV, aligned(1 - core, SPAN)] = got[:QKV, aligned(seq, SPAN)]
        rows = pl.ds(pl.multiple_of(QKV + seq * TILES, TILES), TILES)
        out[QKV:, :WIDTH] = keep[rows, :WIDTH] + got[rows, :WIDTH]


def causal_bias():
    key = lax.broadcasted_iota(jnp.int32, (WIDE, WIDE), 0)
    query = lax.broadcasted_iota(jnp.int32, (WIDE, WIDE), 1)
    return jnp.where(key <= query, 0.0, masked_score).astype(f32)


def biased(score, bias, kb, qb):
    lanes = slice(qb * WIDE, (qb + 1) * WIDE)
    per = WIDE // BLOCK
    parts = []
    for t in range(per):
        row = bias[kb * per + t : kb * per + t + 1, lanes]
        parts.append(score[t * BLOCK : (t + 1) * BLOCK] + row)
    score = jnp.concatenate(parts, axis=0)
    if kb == qb:
        score = score + causal_bias()
    return score


def span_of(b):
    return slice(b * WIDE, (b + 1) * WIDE)


def forward_kernel(*refs):
    pieces, refs = refs[:YS], refs[YS:]
    turned, bias, norm, whole, kv, outs = *refs[:5], refs[5 : 5 + YS]
    qpad, member, scores = refs[5 + YS :]
    y, _, _, _ = place()

    @pl.when(y < SEQS)
    def _():
        member[...] = jnp.zeros_like(member)
        for s, piece in enumerate(pieces):
            turned[:, aligned((y + YS - s) % YS, PAIR)] = piece[:QKV]
            member[...] += piece[QKV:, :BLOCK].astype(f32)
        tile = lax.broadcasted_iota(jnp.int32, (BLOCK, LEN), 0)
        lane = lax.broadcasted_iota(jnp.int32, (BLOCK, LEN), 1) // BLOCK
        spread = jnp.where(tile == lane, 1.0, 0.0).astype(bf16)
        here = dot(member[...].astype(bf16), spread)
        bias[...] = jnp.where(here > 0.5, 0.0, masked_score)
        qpad[:HEAD_DIM] = turned[:HEAD_DIM]
        qpad[HEAD_DIM:] = jnp.zeros((HEAD_DIM, LEN), bf16)
        for b in range(LEN // WIDE):
            kv[span_of(b)] = turned[HEAD_DIM:, span_of(b)].T
        for qb in range(LEN // WIDE):
            qs = span_of(qb)
            query = qpad[:, qs]
            top = jnp.full((1, WIDE), 2 * masked_score, f32)
            for kb in range(qb + 1):
                score = biased(dot(kv[span_of(kb)], query), bias, kb, qb)
                scores[span_of(kb)] = score
                top = jnp.maximum(top, jnp.max(score, axis=0, keepdims=True))
            total = jnp.zeros((1, WIDE), f32)
            acc = jnp.zeros((HEAD_DIM, WIDE), f32)
            for kb in range(qb + 1):
                probs = jnp.exp(scores[span_of(kb)] - top)
                total += jnp.sum(probs, axis=0, keepdims=True)
                acc += dot(turned[2 * HEAD_DIM :, span_of(kb)], probs.astype(bf16))
            whole[:, qs] = (acc / total).astype(bf16)
            norm[:, qs] = jnp.broadcast_to(top + jnp.log(total), (8, WIDE))
        for s, out in enumerate(outs):
            out[...] = whole[:, aligned((y + s) % YS, PAIR)]


def join_kernel(*refs):
    pieces, blocks, outs = refs[:YS], refs[YS : YS + XS], refs[YS + XS :]
    _, _, _, x = place()
    for piece, out in zip(pieces, outs):
        out[:HEAD_DIM] = piece[...]
        for s, block in enumerate(blocks):
            out[HEAD_DIM:, aligned((x + XS - s) % XS, WIDTH)] = block[...]


def gather_kernel(*refs):
    pieces, out, weight = refs[:YS], refs[YS], refs[YS + 1]
    y, _, _, _ = place()
    for s, piece in enumerate(pieces):
        source = (y + YS - s) % YS
        for block in range(XS):
            cols = slice(block * WIDTH, (block + 1) * WIDTH)
            weight[cols, aligned(source, WIDTH)] = piece[HEAD_DIM:, cols]

        @pl.when(source < SEQS)
        def _():
            seq = seq_of(source)
            for core in range(CORES):
                lanes = pl.ds(pl.multiple_of(core * TOKENS + seq * SPAN, SPAN), SPAN)
                out[:, lanes] = piece[:HEAD_DIM, core * SPAN : (core + 1) * SPAN]


def project_kernel(mine, theirs, *refs):
    gs, (allg, own, p1, p2, p3, allw) = refs[:ZS], refs[ZS:]
    _, core, z, x = place()
    for k in range(YS):
        cols = slice(k * WIDTH, (k + 1) * WIDTH)
        allw[:, aligned(k * CORES + core, WIDTH)] = mine[:, cols]
        allw[:, aligned(k * CORES + 1 - core, WIDTH)] = theirs[:, cols]
    for k in range(ZS):
        allg[aligned((z + ZS - k) % ZS, WIDTH), :] = gs[k][...]
    own[...] = dot(allw[aligned(x, WIDTH), :], allg[...])
    for s, out in enumerate((p1, p2, p3)):
        out[...] = dot(allw[aligned((x + s + 1) % XS, WIDTH), :], allg[...]).astype(bf16)


def cotangent_kernel(own, p1, p2, p3, keep, send, whole):
    _, core, _, _ = place()
    total = own[...] + p1[...].astype(f32) + p2[...].astype(f32) + p3[...].astype(f32)
    whole[...] = total.astype(bf16)
    keep[...] = whole[aligned(core, HEAD_DIM), :]
    send[...] = whole[aligned(1 - core, HEAD_DIM), :]


def spread_kernel(keep, got, *outs):
    y, core, _, _ = place()
    for s, out in enumerate(outs):
        seq = seq_of((y + s) % YS)
        out[:, aligned(core, SPAN)] = keep[:, aligned(seq, SPAN)]
        out[:, aligned(1 - core, SPAN)] = got[:, aligned(seq, SPAN)]


def backward_blocks(blocks, turned, bias, norm, kv, qpad, gpad, delta, sums, result):
    for kb in blocks:
        ks = span_of(kb)
        here = slice((kb - blocks[0]) * WIDE, (kb - blocks[0] + 1) * WIDE)
        key_value = kv[ks]
        key_t = turned[HEAD_DIM : 2 * HEAD_DIM, ks]
        key_acc = jnp.zeros((HEAD_DIM, WIDE), f32)
        value_acc = jnp.zeros((HEAD_DIM, WIDE), f32)
        for qb in range(kb, LEN // WIDE):
            qs = span_of(qb)
            score = biased(dot(key_value, qpad[:, qs]), bias, kb, qb)
            probs = jnp.exp(score - norm[:1, qs])
            dprobs = dot(key_value, gpad[:, qs])
            dscore = (probs * (dprobs - delta[:1, qs])).astype(bf16)
            value_acc += dot(gpad[HEAD_DIM:, qs], probs.astype(bf16), NT)
            key_acc += dot(turned[:HEAD_DIM, qs], dscore, NT)
            part = dot(key_t, dscore)
            if kb == 0:
                sums[:, qs] = part
            else:
                sums[:, qs] += part
        result[:HEAD_DIM, here] = key_acc.astype(bf16)
        result[HEAD_DIM:, here] = value_acc.astype(bf16)


def first_backward_kernel(*refs):
    pieces, (turned, bias, norm, whole, kv) = refs[:YS], refs[YS : YS + 5]
    qpad, gpad, delta, sums, result = refs[YS + 5 :]
    y, _, _, _ = place()

    @pl.when(y < SEQS)
    def _():
        qpad[:HEAD_DIM] = turned[:HEAD_DIM]
        qpad[HEAD_DIM:] = jnp.zeros((HEAD_DIM, LEN), bf16)
        gpad[:HEAD_DIM] = jnp.zeros((HEAD_DIM, LEN), bf16)
        for s, piece in enumerate(pieces):
            gpad[HEAD_DIM:, aligned((y + YS - s) % YS, PAIR)] = piece[...]
        products = gpad[HEAD_DIM:].astype(f32) * whole[...].astype(f32)
        delta[...] = jnp.broadcast_to(jnp.sum(products, axis=0, keepdims=True), (8, LEN))
        backward_blocks(KEYS[0], turned, bias, norm, kv, qpad, gpad, delta, sums, result)


def second_backward_kernel(turned, bias, norm, kv, qpad, gpad, delta, before, sums, result):
    y, _, _, _ = place()

    @pl.when(y < SEQS)
    def _():
        sums[...] = before[...]
        backward_blocks(KEYS[1], turned, bias, norm, kv, qpad, gpad, delta, sums, result)


def last_backward_kernel(turned, bias, norm, kv, qpad, gpad, delta, before, r0, r1, *refs):
    outs, (sums, result, query) = refs[:YS], refs[YS:]
    y, _, _, _ = place()

    @pl.when(y < SEQS)
    def _():
        sums[...] = before[...]
        backward_blocks(KEYS[2], turned, bias, norm, kv, qpad, gpad, delta, sums, result)
        query[...] = (sums[...] * HEAD_DIM ** (-0.5)).astype(bf16)
        for s, out in enumerate(outs):
            chunk = (y + s) % YS
            out[:HEAD_DIM] = query[:, aligned(chunk, PAIR)]
            for part, blocks in zip((r0, r1, result), KEYS):
                for block in blocks:
                    lane = (block - blocks[0]) * WIDE
                    slot = block % 2 * WIDE

                    @pl.when(chunk == block // 2)
                    def _():
                        out[HEAD_DIM:, slot : slot + WIDE] = part[:, lane : lane + WIDE]


def collect_kernel(*refs):
    pieces, keep, send = refs[:YS], refs[YS], refs[YS + 1]
    y, core, _, _ = place()
    for s, piece in enumerate(pieces):
        source = (y + YS - s) % YS

        @pl.when(source < SEQS)
        def _():
            lanes = aligned(seq_of(source), SPAN)
            keep[:, lanes] = piece[:, aligned(core, SPAN)]
            send[:, lanes] = piece[:, aligned(1 - core, SPAN)]


def finish_kernel(keep, got, q, k, v, whole):
    _, core, _, _ = place()
    for part, out in enumerate((q, k, v)):
        rows = slice(part * HEAD_DIM, (part + 1) * HEAD_DIM)
        whole[part, aligned(core, HEAD_DIM), :] = keep[rows, :]
        whole[part, aligned(1 - core, HEAD_DIM), :] = got[rows, :]
        out[...] = whole[part].T


def weight_grad_kernel(mine, theirs, o0, o1, o2, o3, *refs):
    outs, allg, allo, product = refs[:YS], refs[YS], refs[YS + 1], refs[YS + 2]
    y, core, _, x = place()
    for s, piece in enumerate((o0, o1, o2, o3)):
        allo[aligned((x + XS - s) % XS, HEAD_DIM), :] = piece[...]
    allg[:, aligned(core, TOKENS)] = mine[...]
    allg[:, aligned(1 - core, TOKENS)] = theirs[...]
    product[...] = dot(allg[...], allo[...], NT)
    for s, out in enumerate(outs):
        out[...] = product[aligned((y + s) % YS, CORES * WIDTH), :].astype(out.dtype)


def total_kernel(*refs):
    parts, (keep, send, whole) = refs[:YS], refs[YS:]
    _, core, _, _ = place()
    total = parts[0][...]
    for part in parts[1:]:
        total = total + part[...].astype(f32)
    whole[...] = total
    square = jnp.sum(jnp.sum(total * total, axis=0, keepdims=True), axis=1, keepdims=True)
    for half, out in ((core, keep), (1 - core, send)):
        out[:WIDTH] = whole[aligned(half, WIDTH), :]
        out[WIDTH:] = jnp.broadcast_to(square, (8, XS * HEAD_DIM))


def square_kernel(keep, got, *refs):
    outs, whole = refs[:XS], refs[XS]
    _, core, _, x = place()
    first = core == 0
    for block in range(XS):
        cols = slice(block * HEAD_DIM, (block + 1) * HEAD_DIM)
        a, b = keep[:WIDTH, cols], got[:WIDTH, cols]
        low, high = jnp.where(first, a, b), jnp.where(first, b, a)
        whole[:, block * WIDTH : (block + 1) * WIDTH] = jnp.concatenate([low, high], axis=1)
    values = whole[...]
    row_sum = lax.dot_general(
        jnp.ones((8, XS * WIDTH), f32),
        values * values,
        NT,
        precision=lax.Precision.HIGHEST,
        preferred_element_type=f32,
    )
    square = keep[WIDTH:, :WIDTH] + got[WIDTH:, :WIDTH]
    for s, out in enumerate(outs):
        out[:WIDTH] = whole[:, aligned((x + s) % XS, WIDTH)]
        out[WIDTH : WIDTH + 8] = row_sum
        out[WIDTH + 8 :] = square


def place_kernel(*refs):
    parts, (moment, grad, rows, cols) = refs[:XS], refs[XS:]
    _, _, _, x = place()
    square = jnp.zeros((8, WIDTH), f32)
    col = jnp.zeros((1, WIDTH), f32)
    for s, part in enumerate(parts):
        source = (x + XS - s) % XS
        values = part[:WIDTH]
        grad[aligned(source, WIDTH), :] = values
        rows[:, aligned(source, WIDTH)] = part[WIDTH : WIDTH + 8]
        square = square + part[WIDTH + 8 :]
        col = col + jnp.sum(values * values, axis=0, keepdims=True)
    rows[:, XS * WIDTH :] = square
    cols[:, :WIDTH] = jnp.broadcast_to(col, (8, WIDTH))
    held = jnp.sum(moment[...], axis=1, keepdims=True)
    cols[:, WIDTH:] = jnp.broadcast_to(held, (8, WIDTH))


def reduce_kernel(r0, r1, c0, c1, rows, cols):
    row = r0[...] + r1[...]
    rows[...] = row[:, : XS * WIDTH]
    cols[:, : 2 * WIDTH] = c0[...] + c1[...]
    cols[:, 2 * WIDTH :] = row[:, XS * WIDTH :]


def update_kernel(c0, c1, c2, c3, rows, grad, row_moment, col_moment, out, new_row, new_col):
    keep = 1.0 - moment_decay
    col = c0[...] + c1[...] + c2[...] + c3[...]
    row_square = rows[:1] / HD + square_floor
    col_square = col[:1, :WIDTH] / D + square_floor
    new_row[...] = moment_decay * row_moment[...] + keep * row_square
    new_col[...] = moment_decay * col_moment[...] + keep * col_square
    held, total = col[:1, WIDTH : 2 * WIDTH], col[:1, 2 * WIDTH :]
    mean = (moment_decay * held + keep * (total / HD + D * square_floor)) / D
    row = jnp.broadcast_to(new_row[...], (8, new_row.shape[1])).T[:, :1]
    out[...] = grad[...] * lax.rsqrt(row * new_col[...] / mean)


def together(arrays):
    return list(lax.optimization_barrier(tuple(arrays)))


def after(arrays, first):
    return together([*arrays, first])[:-1]


def body(queries, keys, values, grad_out, out_weight, tile_plan, row_moment, col_moment):
    flat = lambda a: a.reshape(TOKENS, WIDTH)
    ys = range(1, YS)
    xs = range(1, XS)

    turned, *pieces, keep, send = call(
        pack_kernel,
        [((WIDTH, TOKENS), bf16)]
        + [((WIDTH, WIDTH), bf16)] * XS
        + [((QKV + SEQS * TILES, TOKENS), bf16)] * 2,
        (flat(grad_out), out_weight, flat(queries), flat(keys), flat(values), tile_plan.T),
        scratch=[
            pltpu.VMEM((3 * WIDTH, TOKENS), bf16),
            pltpu.SemaphoreType.DMA((6,)),
            pltpu.VMEM((TOKENS, WIDTH), bf16),
            pltpu.VMEM((XS * WIDTH, WIDTH), bf16),
        ]
        + [pltpu.VMEM((TOKENS, WIDTH), bf16)] * 3
        + [pltpu.VMEM(tile_plan.shape[::-1], jnp.int32)],
        hbm=6,
        limit=61,
    )

    got = swap_core(send)
    packed = call(merge_kernel, [((QKV + TILES, PAIR), bf16)] * YS, (keep, got))
    turned, *packed = together([turned, *packed])
    packed = [packed[0]] + [send_y(packed[s], s) for s in ys]
    up, down = [turned, send_z(turned, 1)], [turned, send_z(turned, -1)]
    up.append(send_z(up[1], 1))
    down.append(send_z(down[1], -1))
    up.append(send_z(up[2], 1))
    down.append(send_z(down[2], -1))
    features = up + [send_z(up[3], 1)] + down[:0:-1]

    pieces = after(pieces, packed[1])
    packed = together([*packed, up[1], down[1]])[:YS]
    pieces = [pieces[0]] + [send_x(pieces[s], s) for s in xs]

    held = call(
        forward_kernel,
        [
            ((QKV, LEN), bf16),
            ((TILES, LEN), f32),
            ((8, LEN), f32),
            ((HEAD_DIM, LEN), bf16),
            ((LEN, 2 * HEAD_DIM), bf16),
        ]
        + [((HEAD_DIM, PAIR), bf16)] * YS,
        (*packed,),
        scratch=[
            pltpu.VMEM((2 * HEAD_DIM, LEN), bf16),
            pltpu.VMEM((TILES, BLOCK), f32),
            pltpu.VMEM((LEN, WIDE), f32),
        ],
        us=6.0,
    )
    held, outputs = held[:5], held[5:]

    outputs = call(
        join_kernel, [((HEAD_DIM + WIDTH, PAIR), bf16)] * YS, (*outputs, *pieces)
    )
    outputs = together([*outputs, up[2], down[2]])[:YS]
    outputs = [outputs[0]] + [send_y(outputs[s], s) for s in ys]
    outputs = together([*outputs, up[3], down[3]])[:YS]
    attn_out, weight = call(
        gather_kernel,
        [((HEAD_DIM, CORES * TOKENS), bf16), ((XS * WIDTH, YS * WIDTH), bf16)],
        (*outputs,),
    )
    attn_outs = [attn_out] + [send_x(attn_out, s) for s in xs]
    weights = [weight, swap_core(weight)]
    weights = together([*weights, *attn_outs[1:]])[:2]

    allg, *partial = call(
        project_kernel,
        [((ZS * WIDTH, TOKENS), bf16), ((WIDTH, TOKENS), f32)] + [((WIDTH, TOKENS), bf16)] * 3,
        (*weights, *features),
        scratch=[pltpu.VMEM((XS * WIDTH, ROWS * WIDTH), bf16)],
    )
    theirs = swap_core(allg)
    partial = [partial[0]] + [send_x(partial[s], s) for s in xs]
    keep, send = call(
        cotangent_kernel,
        [((HEAD_DIM, TOKENS), bf16)] * 2,
        (*partial,),
        scratch=[pltpu.VMEM((WIDTH, TOKENS), bf16)],
    )
    grads = call(spread_kernel, [((HEAD_DIM, PAIR), bf16)] * YS, (keep, swap_core(send)))
    grads = [grads[0]] + [send_y(grads[s], s) for s in ys]

    block = (CORES * WIDTH, XS * HEAD_DIM)
    products = call(
        weight_grad_kernel,
        [(block, f32)] + [(block, bf16)] * (YS - 1),
        (allg, theirs, *attn_outs),
        scratch=[
            pltpu.VMEM((ZS * WIDTH, CORES * TOKENS), bf16),
            pltpu.VMEM((XS * HEAD_DIM, CORES * TOKENS), bf16),
            pltpu.VMEM((ZS * WIDTH, XS * HEAD_DIM), f32),
        ],
        limit=24,
        us=12.0,
    )
    products = [products[0]] + [send_y(products[s], s) for s in ys]
    keep, send = call(
        total_kernel,
        [((WIDTH + 8, XS * HEAD_DIM), f32)] * 2,
        (*products,),
        scratch=[pltpu.VMEM(block, f32)],
    )
    squares = call(
        square_kernel,
        [((WIDTH + 16, WIDTH), f32)] * XS,
        (keep, swap_core(send)),
        scratch=[pltpu.VMEM((WIDTH, XS * WIDTH), f32)],
    )
    squares = [squares[0]] + [send_x(squares[s], s) for s in xs]
    turned, bias, norm, whole, kv = held
    sizes = [len(blocks) * WIDE for blocks in KEYS]
    qpad, gpad, delta, sums, first = call(
        first_backward_kernel,
        [
            ((2 * HEAD_DIM, LEN), bf16),
            ((2 * HEAD_DIM, LEN), bf16),
            ((8, LEN), f32),
            ((HEAD_DIM, LEN), f32),
            ((2 * HEAD_DIM, sizes[0]), bf16),
        ],
        (*grads, *held),
        us=4.0,
    )
    shared = (turned, bias, norm, kv, qpad, gpad, delta)
    squares = after(squares, sums)
    row_held = row_moment.reshape(1, -1)
    weight_grad, row_part, col_part = call(
        place_kernel,
        [((XS * WIDTH, WIDTH), f32), ((8, (XS + 1) * WIDTH), f32), ((8, 2 * WIDTH), f32)],
        (*squares, row_held),
    )


    col_other = swap_core(col_part)
    row_other = swap_z(row_part, 4)
    sums, *_ = together([sums, row_part, col_other])
    sums, second = call(
        second_backward_kernel,
        [((HEAD_DIM, LEN), f32), ((2 * HEAD_DIM, sizes[1]), bf16)],
        (*shared, sums),
        us=4.0,
    )
    row_part = row_part + row_other
    row_other = swap_z(row_part, 2)
    sums = after([sums], row_part)[0]
    results = call(
        last_backward_kernel,
        [((QKV, PAIR), bf16)] * YS,
        (*shared, sums, first, second),
        scratch=[
            pltpu.VMEM((HEAD_DIM, LEN), f32),
            pltpu.VMEM((2 * HEAD_DIM, sizes[2]), bf16),
            pltpu.VMEM((HEAD_DIM, LEN), bf16),
        ],
        us=4.0,
    )
    row_part = row_part + row_other
    results = after(results, row_part)
    row_other = swap_z(row_part, 1)
    row_sum, col_part = call(
        reduce_kernel,
        [((8, XS * WIDTH), f32), ((8, 3 * WIDTH), f32)],
        (row_part, row_other, col_part, col_other),
    )
    col_parts = [col_part] + [send_y(col_part, s) for s in ys]
    results = [results[0]] + [send_y(results[s], s) for s in ys]
    results = after(results, row_sum)
    keep, send = call(collect_kernel, [((QKV, TOKENS), bf16)] * 2, (*results,))
    query_grad, key_grad, value_grad = call(
        finish_kernel,
        [((TOKENS, WIDTH), bf16)] * 3,
        (keep, swap_core(send)),
        scratch=[pltpu.VMEM((3, WIDTH, TOKENS), bf16)],
    )

    update, new_row, new_col = call(
        update_kernel,
        [((XS * WIDTH, WIDTH), f32), ((1, XS * WIDTH), f32), ((1, WIDTH), f32)],
        (*col_parts, row_sum, weight_grad, row_held, col_moment.reshape(1, -1)),
    )
    return (
        query_grad.reshape(queries.shape),
        key_grad.reshape(keys.shape),
        value_grad.reshape(values.shape),
        update,
        new_row.reshape(-1),
        new_col.reshape(-1),
    )


def solution(mesh):
    in_specs = (
        P(None, "row", "col"),
        P(None, "row", "col"),
        P(None, "row", "col"),
        P(None, "row", "col"),
        P("row", "col"),
        P("row", None),
        P("row"),
        P("col"),
    )
    out_specs = (
        P(None, "row", "col"),
        P(None, "row", "col"),
        P(None, "row", "col"),
        P("row", "col"),
        P("row"),
        P("col"),
    )
    return jax.shard_map(body, mesh=mesh, in_specs=in_specs, out_specs=out_specs, check_vma=False)
```
